128 devices in a mesh: dp: 16 (over y_hi, x, core), tensor: 8 (over z, y_lo).
Axes of the slice: x: 4, y: 4 (y_hi: 2, y_lo: 2; y = y_hi * 2 + y_lo), z: 4, core: 2. Of those that a mesh axis runs over, the one named last changes fastest.
Arguments:
- tokens: bfloat16 [16384, 2048], P(('dp', 'tensor')), may hold values from -24 to 24
- segments: int32 [16384], P('dp'), may hold values from 0 to 128, as said below
- cotangent: bfloat16 [16384, 2048], P(('dp', 'tensor')), may hold values from -24 to 24
- attn_gain: float32 [2048], P(('dp', 'tensor')), may hold values from 0.5 to 1.5
- w_query: bfloat16 [2048, 2048], P('dp', 'tensor'), may hold values from -0.125 to 0.125
- w_key: bfloat16 [2048, 2048], P('dp', 'tensor'), may hold values from -0.125 to 0.125
- w_value: bfloat16 [2048, 2048], P('dp', 'tensor'), may hold values from -0.125 to 0.125
- w_beta: bfloat16 [2048, 16], P('dp', 'tensor'), may hold values from -0.125 to 0.125
- conv_weight: bfloat16 [3, 4, 16, 128], P(None, None, 'tensor', 'dp'), may hold values from -3 to 3
- w_out: bfloat16 [2048, 2048], P('tensor', 'dp'), may hold values from -0.25 to 0.25
- ffn_gain: float32 [2048], P(('dp', 'tensor')), may hold values from 0.5 to 1.5
- w_gate: bfloat16 [2048, 5632], P('dp', 'tensor'), may hold values from -0.125 to 0.125
- w_up: bfloat16 [2048, 5632], P('dp', 'tensor'), may hold values from -0.125 to 0.125
- w_down: bfloat16 [5632, 2048], P('tensor', 'dp'), may hold values from -0.078125 to 0.078125
Outputs:
- output: bfloat16 [16384, 2048], P(('dp', 'tensor'))
- tokens_grad: float32 [16384, 2048], P(('dp', 'tensor'))
- attn_gain_grad: float32 [2048], P(('dp', 'tensor'))
- w_query_grad: float32 [2048, 2048], P('dp', 'tensor')
- w_key_grad: float32 [2048, 2048], P('dp', 'tensor')
- w_value_grad: float32 [2048, 2048], P('dp', 'tensor')
- w_beta_grad: float32 [2048, 16], P('dp', 'tensor')
- conv_weight_grad: float32 [3, 4, 16, 128], P(None, None, 'tensor', 'dp')
- w_out_grad: float32 [2048, 2048], P('tensor', 'dp')
- ffn_gain_grad: float32 [2048], P(('dp', 'tensor'))
- w_gate_grad: float32 [2048, 5632], P('dp', 'tensor')
- w_up_grad: float32 [2048, 5632], P('dp', 'tensor')
- w_down_grad: float32 [5632, 2048], P('tensor', 'dp')
The draws below stay inside these ranges and needn't reach their ends.
Inputs may be any that keep to these rules, and one draw needn't show every extreme that they name: Within each sequence of 1024 consecutive tokens, segments start at 0 and rise by 0 or 1 from one token to the next; a rise marks a document start. Each sequence holds one document of at least 896 tokens.
All inputs are finite; a program needn't handle non-finite values.
Results may differ from the reference program's by a relative error of at most 0.02.
Values may be sent and summed in bfloat16 or wider, within the bound.
No kernel may reach another device: no remote copies, remote signals or barrier semaphores. Data moves between devices by JAX's collectives and lax.ppermute only.
A program may use at most 192 MiB of HBM per device.

```python
import jax
import jax.numpy as jnp
from jax import lax

D = 2048
H = 16
DK = 128
FF = 5632
CONV = 4
SPAN = 64
SEQ_LEN = 1024
TOKENS = 16384
ROWS = 128


def draw_segments(key, part):
    key = jax.random.fold_in(key, 11)
    first_key, second_key, third_key, fourth_key = jax.random.split(key, 4)
    count = TOKENS // SEQ_LEN
    opening = jax.random.randint(first_key, (count, 1), 1, ROWS // 2 + 1)
    closing = SEQ_LEN - jax.random.randint(second_key, (count, 1), 1, ROWS // 2 + 1)
    chosen = jax.random.randint(fourth_key, (), 0, count)
    picked = jnp.arange(count, dtype=jnp.int32)[:, None] == chosen
    opening = jnp.where(picked, ROWS // 2, opening)
    closing = jnp.where(picked, SEQ_LEN - ROWS // 2, closing)
    position = jnp.arange(SEQ_LEN, dtype=jnp.int32)[None, :]
    coin_flips = (jax.random.randint(third_key, (count, SEQ_LEN), 0, 6) == 0) | picked
    outside = (position < opening) | (position > closing)
    starts = (position == opening) | (position == closing) | coin_flips & outside
    starts = starts & (position > 0)
    return jnp.cumsum(starts.astype(jnp.int32), axis=1).reshape(count * SEQ_LEN)


def strengthened(values, key, source, target, parts, factor):
    def block_of(dim):
        return (jnp.arange(values.shape[dim]) // (values.shape[dim] // parts)).reshape((-1,) + (1,) * (values.ndim - 1 - dim))

    near = jax.random.permutation(key, parts)[block_of(target)]
    far = (block_of(target) + parts // 2) % parts
    return jnp.where((block_of(source) == near) | (block_of(source) == far), factor * values, values)


def steps_of(key, extent, shards, smallest, largest):
    def one(axis_at, shards_of):
        heights = jax.random.uniform(jax.random.fold_in(jax.random.fold_in(key, 6), axis_at), (shards_of,), jnp.float32, smallest / len(shards), largest / len(shards))
        return jnp.repeat(jnp.exp(heights), extent[axis_at] // shards_of).reshape((-1,) + (1,) * (len(extent) - axis_at - 1))

    level = one(*shards[0])
    for cut in shards[1:]:
        level = level * one(*cut)
    return level


def normal_values(rng, dims, scale, bound, shards=(), kind=jnp.bfloat16):
    level = steps_of(rng, dims, shards, -0.22, 0.18) if shards else 1.0
    values = jax.random.normal(rng, dims, jnp.float32) * scale * level
    return jnp.minimum(jnp.maximum(values, -bound), bound).astype(kind)


def bell_draw_with(own_key, dims, scale, most, pieces, heavy, kind=jnp.bfloat16):
    drawn = scale * jax.random.normal(own_key, dims, jnp.float32)
    if pieces:
        drawn = drawn * steps_of(own_key, dims, pieces, -0.22, 0.18)
    return jnp.clip(strengthened(drawn, jax.random.fold_in(own_key, 3), *heavy), -most, most).astype(kind)


def setup_inputs(seed: int = 0) -> dict:
    streams_of = jax.random.split(jax.random.key(seed), 15)
    return {
        "tokens": bell_draw_with(streams_of[0], (TOKENS, D), 1.0, 24.0, ((0, 128),), (0, 1, 128, 5.5)),
        "segments": draw_segments(jax.random.fold_in(streams_of[14], 71), 0),
        "cotangent": bell_draw_with(streams_of[2], (TOKENS, D), 1.0, 24.0, ((0, 128),), (0, 1, 128, 5.5)),
        "attn_gain": jnp.clip(1.0 + 0.1 * jax.random.normal(streams_of[3], (D,), jnp.float32), 0.5, 1.5),
        "w_query": normal_values(streams_of[4], (D, D), D ** -0.5, 0.125, ((0, 16), (1, 8))),
        "w_key": normal_values(streams_of[5], (D, D), D ** -0.5, 0.125, ((0, 16), (1, 8))),
        "w_value": normal_values(streams_of[6], (D, D), D ** -0.5, 0.125, ((0, 16), (1, 8))),
        "w_beta": normal_values(streams_of[7], (D, H), D ** -0.5, 0.125, ((0, 16), (1, 8))),
        "conv_weight": normal_values(streams_of[8], (3, CONV, H, DK), CONV ** -0.5, 3.0, ((2, 8), (3, 16))),
        "w_out": normal_values(streams_of[9], (D, D), (D // 4) ** -0.5, 0.25, ((0, 8), (1, 16))),
        "ffn_gain": jnp.clip(1.0 + 0.1 * jax.random.normal(streams_of[10], (D,), jnp.float32), 0.5, 1.5),
        "w_gate": normal_values(streams_of[11], (D, FF), D ** -0.5, 0.125, ((0, 16), (1, 8))),
        "w_up": normal_values(streams_of[12], (D, FF), D ** -0.5, 0.125, ((0, 16), (1, 8))),
        "w_down": normal_values(streams_of[13], (FF, D), FF ** -0.5, 0.078125, ((0, 8), (1, 16))),
    }


EPS = 1e-06
PRECISION_FULL = lax.Precision.HIGHEST

@jax.custom_vjp
def low(v):
    return lax.optimization_barrier(v.astype(jnp.bfloat16)).astype(jnp.float32)

@jax.custom_vjp
def low_back(v):
    return v

def low_keep(v):
    return (low(v), None)

def low_pass(kept, grad):
    return (grad,)

def back_keep(v):
    return (v, None)

def back_low(kept, grad):
    return (low(grad),)
low.defvjp(low_keep, low_pass)
low_back.defvjp(back_keep, back_low)

def causal_conv(signal, conv_taps, segs):
    length = signal.shape[0]
    summed = conv_taps[0] * signal
    for offset in range(1, conv_taps.shape[0]):
        shifted = jnp.concatenate([jnp.zeros((offset, signal.shape[1]), jnp.float32), signal[:length - offset]], 0)
        earlier = jnp.concatenate([jnp.full((offset,), -1, jnp.int32), segs[:length - offset]], 0)
        same_doc = (earlier == segs).astype(jnp.float32)[:, None]
        summed = summed + conv_taps[offset] * shifted * same_doc
    return summed

def delta_rule(queries, keys, values, beta, segs, block):
    length, heads, width = queries.shape
    count = length // block

    def blocked(array):
        return array.reshape(count, block, heads, width).transpose(0, 2, 1, 3)
    beta_blocks = beta.reshape(count, block, heads).transpose(0, 2, 1)
    seg_blocks = segs.reshape(count, block)
    previous = jnp.concatenate([jnp.full((1,), -1, jnp.int32), segs[block - 1:length - 1:block]], 0)
    strict_lower = jnp.tril(jnp.ones((block, block), jnp.float32), -1)
    with_diag = jnp.tril(jnp.ones((block, block), jnp.float32), 0)
    identity = jnp.eye(block, dtype=jnp.float32)

    def advance(memory_state, items):
        current_query, current_key, v_now, b_now, s_now, prior = items
        same = (s_now[:, None] == s_now[None, :]).astype(jnp.float32)
        carried = (s_now == prior).astype(jnp.float32)
        gram = jnp.einsum('hik,hjk->hij', current_key, current_key, precision=PRECISION_FULL)
        system = identity + b_now[:, :, None] * gram * same * strict_lower
        retrieved_value = jnp.einsum('jyu,jum->jym', current_key, memory_state, precision=PRECISION_FULL)
        target = b_now[:, :, None] * (v_now - carried[None, :, None] * retrieved_value)
        stored_value = jax.scipy.linalg.solve_triangular(system, target, lower=True, unit_diagonal=True)
        scores = jnp.einsum('hik,hjk->hij', current_query, current_key, precision=PRECISION_FULL) * same * with_diag
        query_output = jnp.einsum('jyu,jum->jym', current_query, memory_state, precision=PRECISION_FULL)
        result = carried[None, :, None] * query_output + jnp.einsum('hij,hjv->hiv', scores, stored_value, precision=PRECISION_FULL)
        closing_state = (s_now == s_now[block - 1]).astype(jnp.float32)
        state_update = jnp.einsum('myq,myd->mqd', current_key * closing_state[None, :, None], stored_value, precision=PRECISION_FULL)
        return (carried[block - 1] * memory_state + state_update, result)
    start_state = jnp.zeros((heads, width, width), jnp.float32)
    final_state, outputs = lax.scan(jax.checkpoint(advance), start_state, (blocked(queries), blocked(keys), blocked(values), beta_blocks, seg_blocks, previous))
    return outputs.transpose(0, 2, 1, 3).reshape(length, heads * width)

def mixer(query_raw, key_raw, value_raw, beta_raw, conv_taps, segs):
    heads = beta_raw.shape[1]
    width = query_raw.shape[1] // heads
    length = query_raw.shape[0]
    conv_rows = conv_taps.reshape(3, conv_taps.shape[1], heads * width)
    queries = jax.nn.silu(causal_conv(query_raw, conv_rows[0], segs)).reshape(length, heads, width)
    keys = jax.nn.silu(causal_conv(key_raw, conv_rows[1], segs)).reshape(length, heads, width)
    values = jax.nn.silu(causal_conv(value_raw, conv_rows[2], segs)).reshape(length, heads, width)
    queries = queries * lax.rsqrt(lax.optimization_barrier(jnp.sum(queries * queries, -1, keepdims=True)) + EPS)
    keys = keys * lax.rsqrt(lax.optimization_barrier(jnp.sum(keys * keys, -1, keepdims=True)) + EPS)
    beta = jax.nn.sigmoid(beta_raw)
    return delta_rule(queries, keys, values, beta, segs, SPAN)

def rms_scale(rows):
    return rows * lax.rsqrt(lax.optimization_barrier(jnp.mean(rows * rows, -1, keepdims=True)) + EPS)

def product(left, right):
    return jnp.dot(left, right, precision=PRECISION_FULL)

def block_forward(rows, segs, attn_gain, w_query, w_key, w_value, w_beta, conv_weight, w_out, ffn_gain, w_gate, w_up, w_down):
    normed = low(rms_scale(rows) * attn_gain)
    query_raw = low_back(product(normed, w_query))
    key_raw = low_back(product(normed, w_key))
    value_raw = low_back(product(normed, w_value))
    beta_raw = low_back(product(normed, w_beta))
    mixed = mixer(query_raw, key_raw, value_raw, beta_raw, conv_weight, segs)
    branch = product(low(mixed), w_out)
    middle = rows + low_back(branch)
    second = low(rms_scale(middle) * ffn_gain)
    gate = low_back(product(second, w_gate))
    up_part = low_back(product(second, w_up))
    active = low(jax.nn.silu(gate) * up_part)
    return middle + product(active, w_down)

def reference(tokens, segments, cotangent, attn_gain, w_query, w_key, w_value, w_beta, conv_weight, w_out, ffn_gain, w_gate, w_up, w_down):
    params = jax.tree.map(lambda item: item.astype(jnp.float32), (attn_gain, w_query, w_key, w_value, w_beta, conv_weight, w_out, ffn_gain, w_gate, w_up, w_down))
    count = tokens.shape[0] // SEQ_LEN
    rows_all = tokens.astype(jnp.float32).reshape(count, SEQ_LEN, D)
    grads_all = cotangent.astype(jnp.float32).reshape(count, SEQ_LEN, D)
    segs_all = segments.reshape(count, SEQ_LEN)

    def one_sequence(sums, items):
        rows, segs, grad_rows = items

        def forward(rows_in, *weights):
            return block_forward(rows_in, segs, *weights)
        result, pullback = jax.vjp(forward, rows, *params)
        grads = pullback(grad_rows)
        sums = jax.tree.map(lambda before, added: before + added, sums, tuple(grads[1:]))
        return (sums, (result, grads[0]))
    zeros = jax.tree.map(jnp.zeros_like, params)
    sums, (outputs, row_grads) = lax.scan(one_sequence, zeros, (rows_all, segs_all, grads_all))
    output = outputs.reshape(count * SEQ_LEN, D).astype(jnp.bfloat16)
    tokens_grad = row_grads.reshape(count * SEQ_LEN, D)
    return (output, tokens_grad, sums[0], sums[1], sums[2], sums[3], sums[4], sums[5], sums[6], sums[7], sums[8], sums[9], sums[10])
```

```python
import functools
import jax
import jax.numpy as jnp
from jax import lax
from jax.experimental import pallas as pl
from jax.experimental.pallas import tpu as pltpu
from jax.sharding import PartitionSpec as P

C = 128
EPS = 1e-06
F32 = jnp.float32
BF16 = jnp.bfloat16
NN = (((1,), (0,)), ((), ()))
NT = (((1,), (1,)), ((), ()))
TN = (((0,), (0,)), ((), ()))


def dot(left, right, dims):
    return lax.dot_general(left, right, dims, preferred_element_type=F32)


def once(left, right, dims):
    return dot(left.astype(BF16), right.astype(BF16), dims)


def halves(value):
    high = value.astype(BF16)
    return high, (value - high.astype(F32)).astype(BF16)


def fine(left, right, dims):
    left_high, left_low = halves(left)
    right_high, right_low = halves(right)
    return (
        dot(left_high, right_high, dims)
        + dot(left_high, right_low, dims)
        + dot(left_low, right_high, dims)
    )


def sigmoid(v):
    return 1.0 / (1.0 + jnp.exp(-v))


def masks():
    row = lax.broadcasted_iota(jnp.int32, (C, C), 0)
    col = lax.broadcasted_iota(jnp.int32, (C, C), 1)
    return row, col


def shifted(rows, before, offset):
    joined = jnp.concatenate([before, rows], 0)
    return pltpu.roll(joined, offset, 0)[8:]


def convolved(rows, before, taps, base, marks):
    total = taps[base : base + 1] * rows
    moved = []
    for offset in range(1, 4):
        term = shifted(rows, before, offset) * marks[offset - 1]
        moved.append(term)
        total = total + taps[base + offset : base + offset + 1] * term
    return total, moved


def inverses(systems):
    row, col = masks()
    eye = jnp.where(row == col, 1.0, 0.0)
    solved = []
    near = (row == col + 1) & ((row & 1) == 1)
    solved = [eye - jnp.where(near, a, 0.0) for a in systems]
    for level in range(1, 7):
        odd = ((row >> level) & 1) == 1
        off = odd & ((row >> level) == (col >> level) + 1)
        parts = [fine(x, jnp.where(off, a, 0.0), NN) for x, a in zip(solved, systems)]
        solved = [x - fine(p, x, NN) for x, p in zip(solved, parts)]
    return solved


def forward_kernel(chunks, mm, raw, taps, aux, segs, mixed, t_out, u_out, s_out, m_out, q_out, before, state):
    step = pl.program_id(0)

    @pl.when(step == 0)
    def _():
        before[...] = jnp.zeros_like(before)
        state[...] = jnp.zeros_like(state)

    row, col = masks()
    eye = jnp.where(row == col, 1.0, 0.0)
    taps_now = taps[...]
    items = []
    for c in range(chunks):
        rows = pl.ds(c * C, C)
        prev = before[...] if c == 0 else raw[pl.ds(c * C - 8, 8), :768]
        marks = [aux[rows, j : j + 1] for j in range(3)]
        carried, closing, seg = aux[rows, 3:4], aux[rows, 4:5], aux[rows, 5:6]
        same = seg == segs[0, c : c + 1, :]
        gamma = carried[C - 1 : C]
        acts = []
        for part in range(3):
            cols = slice(part * 256, part * 256 + 256)
            conv, _ = convolved(raw[rows, cols], prev[:, cols], taps_now, part * 4, marks)
            acts.append(conv * sigmoid(conv))
        for h in range(2):
            hc = slice(h * 128, h * 128 + 128)
            q, k, v = acts[0][:, hc], acts[1][:, hc], acts[2][:, hc]
            q = q * lax.rsqrt(jnp.sum(q * q, -1, keepdims=True) + EPS)
            k = k * lax.rsqrt(jnp.sum(k * k, -1, keepdims=True) + EPS)
            b = sigmoid(raw[rows, 768 + h : 769 + h])
            items.append((q, k, v, b, carried, closing, same, gamma))
    before[...] = raw[pl.ds(chunks * C - 8, 8), :768]
    systems, scores = [], []
    for q, k, v, b, carried, closing, same, gamma in items:
        gram = mm(k, k, NT)
        systems.append(jnp.where(same & (row > col), b * gram, 0.0))
        scores.append(jnp.where(same & (row >= col), mm(q, k, NT), 0.0))
    solved = inverses(systems)
    wus = [
        mm(t, jnp.concatenate([(i[4] * i[3]) * i[1], i[3] * i[2]], 1), NN)
        for t, i in zip(solved, items)
    ]
    mns = [mm(i[5] * i[1], wu, TN) for wu, i in zip(wus, items)]
    qos = [mm(p, wu, NN) for p, wu in zip(scores, wus)]
    for n, i in enumerate(items):
        t_out[n] = solved[n]
        c, h = n // 2, n % 2
        now = state[h]
        s_out[n] = now
        move = i[7] * eye - mns[n][:, :128]
        query = i[4] * i[0] - qos[n][:, :128]
        m_out[n] = move
        q_out[n] = query
        state[h] = mm(move, now, NN) + mns[n][:, 128:]
        u_out[n] = wus[n][:, 128:] - mm(wus[n][:, :128], now, NN)
        mixed[pl.ds(c * C, C), h * 128 : h * 128 + 128] = (mm(query, now, NN) + qos[n][:, 128:]).astype(BF16)


def mix_forward(raw, taps, aux, segs, chunks=2, mm=once):
    steps = 8 // chunks
    saved = jax.ShapeDtypeStruct((16, C, C), F32)
    block = pl.BlockSpec((2 * chunks, C, C), lambda i: (i, 0, 0))
    return pl.pallas_call(
        functools.partial(forward_kernel, chunks, mm),
        grid=(steps,),
        in_specs=[
            pl.BlockSpec((chunks * C, 896), lambda i: (i, 0)),
            pl.BlockSpec((12, 256), lambda i: (0, 0)),
            pl.BlockSpec((chunks * C, 128), lambda i: (i, 0)),
            pl.BlockSpec((1, chunks, 128), lambda i: (i, 0, 0)),
        ],
        out_specs=[pl.BlockSpec((chunks * C, 256), lambda i: (i, 0))] + [block] * 5,
        out_shape=[jax.ShapeDtypeStruct((1024, 256), BF16)] + [saved] * 5,
        scratch_shapes=[pltpu.VMEM((8, 768), F32), pltpu.VMEM((2, C, C), F32)],
        compiler_params=pltpu.CompilerParams(vmem_limit_bytes=48 * 1024 * 1024),
        name="mix_forward",
    )(raw, taps, aux, segs.reshape(steps, chunks, 128))


def backward_kernel(chunks, mm, raw, prior, taps, aux, segs, grad, t_in, u_in, s_in, m_in, q_in, back, taps_grad, after, adjoint):
    step = pl.program_id(0)
    last = pl.num_programs(0) - 1
    back[:, 768:] = jnp.zeros_like(back[:, 768:])

    @pl.when(step == 0)
    def _():
        after[...] = jnp.zeros_like(after)
        adjoint[...] = jnp.zeros_like(adjoint)
        taps_grad[...] = jnp.zeros_like(taps_grad)

    row, col = masks()
    taps_now = taps[...]
    taps_sum = [[jnp.zeros((1, 256), F32) for _ in range(4)] for _ in range(3)]
    items = []
    for c in range(chunks):
        rows = pl.ds(c * C, C)
        if c == 0:
            prev = jnp.where(step == last, 0.0, prior[:, :768])
        else:
            prev = raw[pl.ds(c * C - 8, 8), :768]
        marks = [aux[rows, j : j + 1] for j in range(3)]
        carried, closing, seg = aux[rows, 3:4], aux[rows, 4:5], aux[rows, 5:6]
        same = seg == segs[0, c : c + 1, :]
        acts, slopes, moved = [], [], []
        for part in range(3):
            cols = slice(part * 256, part * 256 + 256)
            now = raw[rows, cols]
            conv, terms = convolved(now, prev[:, cols], taps_now, part * 4, marks)
            s = sigmoid(conv)
            acts.append(conv * s)
            slopes.append(s * (1.0 + conv * (1.0 - s)))
            moved.append([now] + terms)
        heads = []
        for h in range(2):
            hc = slice(h * 128, h * 128 + 128)
            q, k, v = acts[0][:, hc], acts[1][:, hc], acts[2][:, hc]
            rq = lax.rsqrt(jnp.sum(q * q, -1, keepdims=True) + EPS)
            rk = lax.rsqrt(jnp.sum(k * k, -1, keepdims=True) + EPS)
            b = sigmoid(raw[rows, 768 + h : 769 + h])
            heads.append((q * rq, k * rk, v, b, rq, rk, grad[rows, hc]))
        items.append((marks, carried, closing, same, slopes, moved, heads))
    for c in reversed(range(chunks)):
        marks, carried, closing, same, slopes, moved, heads = items[c]
        back_q, back_k, back_v = [], [], []
        for h in range(2):
            n = 2 * c + h
            q, k, v, b, rq, rk, do = heads[h]
            t, u, s, m, qe = t_in[n], u_in[n], s_in[n], m_in[n], q_in[n]
            g = adjoint[h]
            adjoint[h] = mm(m, g, TN) + mm(qe, do, TN)
            gram = mm(k, k, NT)
            score = jnp.where(same & (row >= col), mm(q, k, NT), 0.0)
            du = mm(score, do, TN) + mm(closing * k, g, NN)
            dr = mm(t, du, TN)
            dps = mm(jnp.concatenate([do, dr], 0), u, NT)
            dp = jnp.where(same & (row >= col), dps[:C], 0.0)
            da = jnp.where(same & (row > col), -dps[C:], 0.0)
            e = b * da
            sides = mm(jnp.concatenate([carried * do, (carried * b) * dr], 0), s, NT)
            inner = mm(jnp.concatenate([dp, e], 0), k, NN)
            dq = sides[:C] + inner[:C]
            dk = (
                inner[C:]
                - sides[C:]
                + mm(jnp.concatenate([dp, e], 0), jnp.concatenate([q, k], 0), TN)
                + closing * mm(u, g, NT)
            )
            ks = mm(k, s, NN)
            db = jnp.sum(dr * (v - carried * ks) + da * gram, -1, keepdims=True)
            back_q.append(rq * (dq - q * jnp.sum(dq * q, -1, keepdims=True)))
            back_k.append(rk * (dk - k * jnp.sum(dk * k, -1, keepdims=True)))
            back_v.append(b * dr)
            back[pl.ds(c * C, C), 768 + h : 769 + h] = (db * b * (1.0 - b)).astype(BF16)
        for part, pair in enumerate((back_q, back_k, back_v)):
            d = jnp.concatenate(pair, 1) * slopes[part]
            total = taps_now[part * 4 : part * 4 + 1] * d
            taps_sum[part][0] += jnp.sum(d * moved[part][0], 0, keepdims=True)
            cols = slice(part * 256, part * 256 + 256)
            for offset in range(1, 4):
                taps_sum[part][offset] += jnp.sum(d * moved[part][offset], 0, keepdims=True)
                marked = d * marks[offset - 1]
                joined = jnp.concatenate([marked, after[offset - 1, :, cols]], 0)
                after[offset - 1, :, cols] = marked[:8]
                up = pltpu.roll(joined, C + 8 - offset, 0)[:C]
                total = total + taps_now[part * 4 + offset : part * 4 + offset + 1] * up
            back[pl.ds(c * C, C), cols] = total.astype(BF16)
    for part in range(3):
        for offset in range(4):
            r = part * 4 + offset
            taps_grad[r : r + 1, :] += taps_sum[part][offset]


def mix_backward(raw, taps, aux, segs, grad, saved, chunks=2, mm=once):
    steps = 8 // chunks
    block = pl.BlockSpec((2 * chunks, C, C), lambda i: (steps - 1 - i, 0, 0))
    rows = lambda width: pl.BlockSpec((chunks * C, width), lambda i: (steps - 1 - i, 0))
    return pl.pallas_call(
        functools.partial(backward_kernel, chunks, mm),
        grid=(steps,),
        in_specs=[
            rows(896),
            pl.BlockSpec((8, 896), lambda i: (jnp.maximum((steps - 1 - i) * chunks * 16 - 1, 0), 0)),
            pl.BlockSpec((12, 256), lambda i: (0, 0)),
            rows(128),
            pl.BlockSpec((1, chunks, 128), lambda i: (steps - 1 - i, 0, 0)),
            rows(256),
        ]
        + [block] * 5,
        out_specs=[rows(896), pl.BlockSpec((12, 256), lambda i: (0, 0))],
        out_shape=[
            jax.ShapeDtypeStruct((1024, 896), BF16),
            jax.ShapeDtypeStruct((12, 256), F32),
        ],
        scratch_shapes=[pltpu.VMEM((3, 8, 768), F32), pltpu.VMEM((2, C, C), F32)],
        compiler_params=pltpu.CompilerParams(vmem_limit_bytes=48 * 1024 * 1024),
        name="mix_backward",
    )(raw, raw, taps, aux, segs.reshape(steps, chunks, 128), grad, *saved)


def mix_marks(segs):
    marks = [
        jnp.concatenate([jnp.zeros((o,), F32), (segs[o:] == segs[:-o]).astype(F32)])
        for o in range(1, 4)
    ]
    blocks = segs.reshape(8, C)
    prior = jnp.concatenate([jnp.full((1,), -1, jnp.int32), blocks[:-1, -1]])
    carried = (blocks == prior[:, None]).astype(F32).reshape(1024)
    closing = (blocks == blocks[:, -1:]).astype(F32).reshape(1024)
    columns = jnp.stack(marks + [carried, closing, segs.astype(F32)], 1)
    return jnp.pad(columns, ((0, 0), (0, 122))), blocks.astype(F32)


AXES = ("yh", "x", "c", "z", "yl")
TEAM = ("z", "c")
RING = ("yh", "yl", "x")
PAD = 768
HID = 704


def trade(value):
    return lax.ppermute(value, ("c", "yl"), [(0, 0), (1, 2), (2, 1), (3, 3)])


def mate(value):
    return lax.ppermute(value, "c", [(0, 1), (1, 0)])


def ordered(rows):
    count = rows.shape[0]
    return rows.reshape(count, 2, 4, 2, 128).transpose(0, 1, 3, 2, 4).reshape(count, 2048)


def restored(rows):
    count = rows.shape[0]
    return rows.reshape(count, 2, 2, 4, 128).transpose(0, 1, 3, 2, 4).reshape(count, 2048)


def gather_team(rows):
    return lax.all_gather(rows, TEAM, axis=0, tiled=True)


def sum_team(part):
    return lax.psum_scatter(part, TEAM, scatter_dimension=0, tiled=True).astype(F32)


def gather_ring(rows):
    return lax.all_gather(rows, RING, axis=0, tiled=True)


def sum_ring(part):
    return lax.psum_scatter(part, RING, scatter_dimension=0, tiled=True)


def matmul(left, right, dims, kind=F32):
    return lax.dot_general(left, right, dims, preferred_element_type=F32).astype(kind)


def inverse_rms(rows):
    return lax.rsqrt(jnp.mean(rows * rows, -1, keepdims=True) + EPS)


def norm_back(normed, scale, scaled):
    return scale * (scaled - normed * jnp.mean(scaled * normed, -1, keepdims=True))


def on_device(
    tokens,
    segments,
    cotangent,
    attn_gain,
    w_query,
    w_key,
    w_value,
    w_beta,
    conv_weight,
    w_out,
    ffn_gain,
    w_gate,
    w_up,
    w_down,
):
    gains = jnp.broadcast_to(jnp.stack([attn_gain, ffn_gain])[None], (8, 2, 16))
    gains = lax.all_to_all(gains, ("z", "yl"), 0, 0, tiled=True).transpose(1, 0, 2).reshape(2, 128, 1)
    gain_one, gain_two = gains[0], gains[1]

    rows = ordered(trade(tokens)).astype(F32)
    scale_one = inverse_rms(rows)
    normed_one = rows * scale_one
    seq_one = gather_team(normed_one.astype(BF16))

    def scaled(weight, gain):
        return (weight.astype(F32) * gain).astype(BF16)

    taps_block = jnp.pad(conv_weight.reshape(24, 8), ((0, 104), (0, 112)))
    small = jnp.concatenate([jnp.pad(scaled(w_beta, gain_one), ((0, 0), (0, 6))), taps_block], 1)
    mix_pack = jnp.concatenate(
        [scaled(w, gain_one) for w in (w_query, w_key, w_value)] + [small, w_out.T], 1
    )
    wide = ((0, 0), (0, PAD - HID))
    ffn_pack = jnp.concatenate(
        [jnp.pad(scaled(w, gain_two), wide) for w in (w_gate, w_up)] + [jnp.pad(w_down.T, wide)], 1
    )
    mix_w = gather_ring(trade(mix_pack))
    in_w, out_w = mix_w[:, :896], mix_w[:, 896:]
    ffn_w = gather_ring(trade(ffn_pack))
    gate_up_w, down_w = ffn_w[:, : 2 * PAD], ffn_w[:, 2 * PAD :]
    taps = in_w[:, 768:].reshape(2, 2, 4, 128, 128)[:, :, :, :24, 8:16]
    taps = taps.transpose(3, 0, 2, 1, 4).reshape(12, 256).astype(F32)
    own = lax.axis_index("c") == lax.axis_index("yl")
    segs = jnp.where(own, segments, mate(segments))
    marks, seg_rows = mix_marks(segs)

    raw = matmul(seq_one, in_w, NN)
    mixed, *saved = mix_forward(raw, taps, marks, seg_rows, chunks=4, mm=fine)
    middle = rows + sum_team(matmul(mixed, out_w, NT, BF16))
    scale_two = inverse_rms(middle)
    normed_two = middle * scale_two
    seq_two = gather_team(normed_two.astype(BF16))
    grad_rows = ordered(trade(cotangent))
    seq_grad = gather_team(grad_rows)
    grad_active = matmul(seq_grad, down_w, NN)
    gate_up = matmul(seq_two, gate_up_w, NN)
    gate, up_part = gate_up[:, :PAD], gate_up[:, PAD:]
    sigma = sigmoid(gate)
    swish = gate * sigma
    active = (swish * up_part).astype(BF16)
    slope = sigma * (1.0 + gate * (1.0 - sigma))
    both_back = jnp.concatenate([grad_active * up_part * slope, grad_active * swish], 1).astype(BF16)
    second = sum_team(matmul(both_back, gate_up_w, NT, BF16))
    middle_grad = grad_rows.astype(F32) + norm_back(normed_two, scale_two, second)
    seq_middle = gather_team(middle_grad.astype(BF16))
    result = middle + sum_team(matmul(active, down_w, NT, BF16))
    output = trade(restored(result.astype(BF16)))
    ffn_grad = jnp.concatenate([matmul(seq_two, both_back, TN, BF16), matmul(seq_grad, active, TN, BF16)], 1)
    ffn_grad = trade(sum_ring(ffn_grad)).astype(F32)

    mixed_back = matmul(seq_middle, out_w, NN)
    back, taps_grad = mix_backward(raw, taps, marks, seg_rows, mixed_back, saved, chunks=2, mm=fine)
    first = sum_team(matmul(back, in_w, NT, BF16))
    tokens_grad = middle_grad + norm_back(normed_one, scale_one, first)
    tokens_grad = trade(restored(tokens_grad.astype(BF16))).astype(F32)
    taps_grad = taps_grad.reshape(24, 2, 4, 2, 8).transpose(1, 3, 2, 0, 4).reshape(16, 24, 8).astype(BF16)
    taps_grad = jnp.pad(taps_grad, ((0, 0), (0, 104), (8, 112))).reshape(2048, 128)
    in_grad = matmul(seq_one, back, TN, BF16)
    mix_grad = jnp.concatenate(
        [in_grad[:, :768], in_grad[:, 768:] + taps_grad, matmul(seq_middle, mixed, TN, BF16)], 1
    )
    mix_grad = trade(sum_ring(mix_grad)).astype(F32)

    grad_query, grad_key, grad_value = (mix_grad[:, n * 256 : n * 256 + 256] for n in range(3))
    grad_beta, grad_taps, grad_out = mix_grad[:, 768:770], mix_grad[:24, 776:784], mix_grad[:, 896:]
    grad_gate, grad_up, grad_down = (ffn_grad[:, n * PAD : n * PAD + HID] for n in range(3))

    def dotted(pairs):
        return sum(jnp.sum(grad * weight.astype(F32), 1) for grad, weight in pairs)

    gain_parts = jnp.stack(
        [
            dotted([(grad_query, w_query), (grad_key, w_key), (grad_value, w_value), (grad_beta, w_beta)]),
            dotted([(grad_gate, w_gate), (grad_up, w_up)]),
        ]
    )
    gain_parts = gain_parts.reshape(2, 8, 16).transpose(1, 0, 2)
    gain_sums = jnp.sum(lax.all_to_all(gain_parts, ("z", "yl"), 0, 0, tiled=True), 0)
    return (
        output,
        tokens_grad,
        gain_sums[0],
        grad_query * gain_one,
        grad_key * gain_one,
        grad_value * gain_one,
        grad_beta * gain_one,
        grad_taps.reshape(3, 4, 2, 8),
        grad_out.T,
        gain_sums[1],
        grad_gate * gain_two,
        grad_up * gain_two,
        grad_down.T,
    )


def solution(mesh):
    dp, tensor = ("yh", "x", "c"), ("z", "yl")
    every = dp + tensor
    split = jax.sharding.Mesh(mesh.devices.reshape(2, 4, 2, 4, 2), AXES)
    placed = (
        P(every, None),
        P(dp),
        P(every, None),
        P(every),
        P(dp, tensor),
        P(dp, tensor),
        P(dp, tensor),
        P(dp, tensor),
        P(None, None, tensor, dp),
        P(tensor, dp),
        P(every),
        P(dp, tensor),
        P(dp, tensor),
        P(tensor, dp),
    )
    return jax.shard_map(
        on_device,
        mesh=split,
        in_specs=placed,
        out_specs=(
            P(every, None),
            P(every, None),
            P(every),
            P(dp, tensor),
            P(dp, tensor),
            P(dp, tensor),
            P(dp, tensor),
            P(None, None, tensor, dp),
            P(tensor, dp),
            P(every),
            P(dp, tensor),
            P(dp, tensor),
            P(tensor, dp),
        ),
        check_vma=False,
    )
```

```python
import functools
import jax
import jax.numpy as jnp
from jax import lax
from jax.experimental import pallas as pl
from jax.experimental.pallas import tpu as pltpu
from jax.sharding import PartitionSpec as P

C = 128
D = 2048
PARTS = (512, 512)
EPS = 1e-06
F32 = jnp.float32
BF16 = jnp.bfloat16
NN = (((1,), (0,)), ((), ()))
NT = (((1,), (1,)), ((), ()))
TN = (((0,), (0,)), ((), ()))


def dot(left, right, dims):
    return lax.dot_general(left, right, dims, preferred_element_type=F32)


def once(left, right, dims):
    return dot(left.astype(BF16), right.astype(BF16), dims)


def halves(value):
    high = value.astype(BF16)
    return high, (value - high.astype(F32)).astype(BF16)


def fine(left, right, dims):
    left_high, left_low = halves(left)
    right_high, right_low = halves(right)
    (over,), (under,) = dims[0]
    first = dot(
        jnp.concatenate([left_high, left_low], over), jnp.concatenate([right_high, right_high], under), dims
    )
    return first + dot(left_high, right_low, dims)


def sigmoid(v):
    return 1.0 / (1.0 + jnp.exp(-v))


def masks():
    row = lax.broadcasted_iota(jnp.int32, (C, C), 0)
    col = lax.broadcasted_iota(jnp.int32, (C, C), 1)
    return row, col


def shifted(rows, before, offset):
    joined = jnp.concatenate([before, rows], 0)
    return pltpu.roll(joined, offset, 0)[8:]


def convolved(rows, before, taps, marks):
    total = taps[0:1] * rows
    moved = []
    for offset in range(1, 4):
        term = shifted(rows, before, offset) * marks[offset - 1]
        moved.append(term)
        total = total + taps[offset : offset + 1] * term
    return total, moved


def inverses(systems):
    row, col = masks()
    eye = jnp.where(row == col, 1.0, 0.0)
    solved = []
    near = (row == col + 1) & ((row & 1) == 1)
    solved = [eye - jnp.where(near, a, 0.0) for a in systems]
    for level in range(1, 7):
        odd = ((row >> level) & 1) == 1
        off = odd & ((row >> level) == (col >> level) + 1)
        parts = [fine(x, jnp.where(off, a, 0.0), NN) for x, a in zip(solved, systems)]
        solved = [x - fine(p, x, NN) for x, p in zip(solved, parts)]
    return solved


def forward_kernel(chunks, mm, place, same, other, weights, out_w, out_w_next, taps, aux, segs, wait, wait_next, mixed, raw, part_same, part_other, t_out, u_out, s_out, m_out, q_out, before, state):
    step = pl.program_id(0)

    @pl.when(step == 0)
    def _():
        raw[:512, :] = dot(same[...], weights[...], NN)
        raw[512:, :] = dot(other[...], weights[...], NN)
        before[...] = jnp.zeros_like(before)
        state[...] = jnp.zeros_like(state)

    row, col = masks()
    eye = jnp.where(row == col, 1.0, 0.0)
    taps_now = taps[...]
    items = []
    for c in range(chunks):
        rows, fixed = spot(place, chunks * step + c), pl.ds(c * C, C)
        prev = before[...] if c == 0 else raw[spot(place, chunks * step + c - 1, 120, 8), :768]
        marks = [aux[fixed, j : j + 1] for j in range(3)]
        carried, closing, seg = aux[fixed, 3:4], aux[fixed, 4:5], aux[fixed, 5:6]
        same_doc = seg == segs[0, c : c + 1, :]
        gamma = carried[C - 1 : C]
        for h in range(2):
            acts = []
            for part in range(3):
                cols = slice(384 * h + 128 * part, 384 * h + 128 * part + 128)
                conv, _ = convolved(raw[rows, cols], prev[:, cols], taps_now[:, cols], marks)
                acts.append(conv * sigmoid(conv))
            q, k, v = acts
            q = q * lax.rsqrt(jnp.sum(q * q, -1, keepdims=True) + EPS)
            k = k * lax.rsqrt(jnp.sum(k * k, -1, keepdims=True) + EPS)
            b = sigmoid(raw[rows, 768 + h : 769 + h])
            items.append((q, k, v, b, carried, closing, same_doc, gamma))
    before[...] = raw[spot(place, chunks * step + chunks - 1, 120, 8), :768]
    systems, scores = [], []
    for q, k, v, b, carried, closing, same_doc, gamma in items:
        gram = mm(k, k, NT)
        systems.append(jnp.where(same_doc & (row > col), b * gram, 0.0))
        scores.append(jnp.where(same_doc & (row >= col), mm(q, k, NT), 0.0))
    solved = inverses(systems)
    wus = [
        mm(t, jnp.concatenate([(i[4] * i[3]) * i[1], i[3] * i[2]], 1), NN)
        for t, i in zip(solved, items)
    ]
    mns = [mm(i[5] * i[1], wu, TN) for wu, i in zip(wus, items)]
    qos = [mm(p, wu, NN) for p, wu in zip(scores, wus)]
    for n, i in enumerate(items):
        c, h = n // 2, n % 2
        t_out[h, c] = solved[n]
        now = state[h]
        s_out[h, c] = now
        move = i[7] * eye - mns[n][:, :128]
        query = i[4] * i[0] - qos[n][:, :128]
        m_out[h, c] = move
        q_out[h, c] = query
        state[h] = mm(move, now, NN) + mns[n][:, 128:]
        u_out[h, c] = wus[n][:, 128:] - mm(wus[n][:, :128], now, NN)
        result = (mm(query, now, NN) + qos[n][:, 128:]).astype(BF16)
        mixed[spot(place, chunks * step + c), h * 128 : h * 128 + 128] = result

    @pl.when(step == pl.num_programs(0) - 1)
    def _():
        project = jnp.concatenate([out_w[...], out_w_next[...]], 1)
        at = 0
        for ref in (part_same, part_other):
            count = ref.shape[0]
            ref[...] = dot(mixed[at : at + count, :], project, NT).astype(BF16)
            at += count


def spot(place, block, start=0, count=C):
    return pl.ds(pl.multiple_of(place[block] * C + start, 8), count)


def mix_forward(place, parts, weights, taps, aux, segs, waits, mm=fine):
    chunks, steps = 4, 2
    saved = jax.ShapeDtypeStruct((2, 8, C, C), F32)
    block = pl.BlockSpec((2, chunks, C, C), lambda i, place: (0, i, 0, 0))
    rows = lambda width: pl.BlockSpec((1024, width), lambda i, place: (0, 0))
    return pl.pallas_call(
        functools.partial(forward_kernel, chunks, mm),
        grid_spec=pltpu.PrefetchScalarGridSpec(
            num_scalar_prefetch=1,
            grid=(steps,),
            in_specs=[
                *[pl.BlockSpec((part.shape[0], D), lambda i, place: (0, 0)) for part in parts],
                pl.BlockSpec((D, 896), lambda i, place: (0, 0)),
                *[pl.BlockSpec((D, 128), lambda i, place, n=n: (0, 7 + n)) for n in range(2)],
                pl.BlockSpec((4, 768), lambda i, place: (0, 0)),
                pl.BlockSpec((chunks * C, 128), lambda i, place: (i, 0)),
                pl.BlockSpec((1, chunks, 128), lambda i, place: (i, 0, 0)),
                *[pl.BlockSpec(memory_space=pl.ANY) for _ in waits],
            ],
            out_specs=[rows(256), rows(896)]
            + [pl.BlockSpec((count, D), lambda i, place: (0, 0)) for count in PARTS]
            + [block] * 5,
            scratch_shapes=[pltpu.VMEM((8, 768), F32), pltpu.VMEM((2, C, C), F32)],
        ),
        out_shape=[jax.ShapeDtypeStruct((1024, 256), BF16)]
        + [jax.ShapeDtypeStruct((1024, 896), F32)]
        + [jax.ShapeDtypeStruct((count, D), BF16) for count in PARTS]
        + [saved] * 5,
        compiler_params=pltpu.CompilerParams(vmem_limit_bytes=48 * 1024 * 1024),
        cost_estimate=pl.CostEstimate(flops=20 << 30, bytes_accessed=20 << 20, transcendentals=0),
        name="mix_forward",
    )(place, *parts, weights, weights, weights, taps, aux, segs.reshape(steps, chunks, 128), *waits)


def backward_kernel(chunks, mm, place, near, other, out_w, out_w_next, raw, taps, aux, segs, t_in, u_in, s_in, m_in, q_in, back, taps_grad, after, adjoint, grad):
    step = pl.program_id(0)
    last = pl.num_programs(0) - 1
    start = chunks * (last - step)

    @pl.when(step == 0)
    def _():
        weights = jnp.concatenate([out_w[...], out_w_next[...]], 1)
        at = 0
        for ref in (near, other):
            grad[at : at + ref.shape[0], :] = dot(ref[...], weights, NN)
            at += ref.shape[0]
        after[...] = jnp.zeros_like(after)
        adjoint[...] = jnp.zeros_like(adjoint)
        taps_grad[...] = jnp.zeros_like(taps_grad)
        back[:, 768:] = jnp.zeros_like(back[:, 768:])

    row, col = masks()
    taps_sum = [[jnp.zeros((1, 128), F32) for _ in range(4)] for _ in range(6)]
    items = []
    for c in range(chunks):
        rows, fixed = spot(place, start + c), pl.ds(c * C, C)
        if c == 0:
            prev = jnp.where(step == last, 0.0, raw[spot(place, jnp.maximum(start - 1, 0), 120, 8), :768])
        else:
            prev = raw[spot(place, start + c - 1, 120, 8), :768]
        marks = [aux[fixed, j : j + 1] for j in range(3)]
        carried, closing, seg = aux[fixed, 3:4], aux[fixed, 4:5], aux[fixed, 5:6]
        same = seg == segs[0, c : c + 1, :]
        for h in range(2):
            acts, slopes, moved = [], [], []
            for part in range(3):
                cols = slice(384 * h + 128 * part, 384 * h + 128 * part + 128)
                now = raw[rows, cols]
                conv, terms = convolved(now, prev[:, cols], taps[:, cols], marks)
                s = sigmoid(conv)
                acts.append(conv * s)
                slopes.append(s * (1.0 + conv * (1.0 - s)))
                moved.append([now] + terms)
            q, k, v = acts
            rq = lax.rsqrt(jnp.sum(q * q, -1, keepdims=True) + EPS)
            rk = lax.rsqrt(jnp.sum(k * k, -1, keepdims=True) + EPS)
            b = sigmoid(raw[rows, 768 + h : 769 + h])
            do = grad[rows, 128 * h : 128 * h + 128]
            items.append((c, h, marks, carried, closing, same, slopes, moved, q * rq, k * rk, v, b, rq, rk, do))
    for item in sorted(items, key=lambda item: (-item[0], item[1])):
        c, h, marks, carried, closing, same, slopes, moved, q, k, v, b, rq, rk, do = item
        t, u, s, m, qe = t_in[h, c], u_in[h, c], s_in[h, c], m_in[h, c], q_in[h, c]
        g = adjoint[h]
        adjoint[h] = mm(m, g, TN) + mm(qe, do, TN)
        gram = mm(k, k, NT)
        score = jnp.where(same & (row >= col), mm(q, k, NT), 0.0)
        du = mm(score, do, TN) + mm(closing * k, g, NN)
        dr = mm(t, du, TN)
        dps = mm(jnp.concatenate([do, dr], 0), u, NT)
        dp = jnp.where(same & (row >= col), dps[:C], 0.0)
        da = jnp.where(same & (row > col), -dps[C:], 0.0)
        e = b * da
        sides = mm(jnp.concatenate([carried * do, (carried * b) * dr], 0), s, NT)
        inner = mm(jnp.concatenate([dp, e], 0), k, NN)
        dq = sides[:C] + inner[:C]
        dk = (
            inner[C:]
            - sides[C:]
            + mm(jnp.concatenate([dp, e], 0), jnp.concatenate([q, k], 0), TN)
            + closing * mm(u, g, NT)
        )
        ks = mm(k, s, NN)
        db = jnp.sum(dr * (v - carried * ks) + da * gram, -1, keepdims=True)
        backs = (
            rq * (dq - q * jnp.sum(dq * q, -1, keepdims=True)),
            rk * (dk - k * jnp.sum(dk * k, -1, keepdims=True)),
            b * dr,
        )
        rows = spot(place, start + c)
        back[rows, 768 + h : 769 + h] = (db * b * (1.0 - b)).astype(BF16)
        for part in range(3):
            d = backs[part] * slopes[part]
            cols = slice(384 * h + part * 128, 384 * h + part * 128 + 128)
            sums = taps_sum[3 * h + part]
            total = taps[0:1, cols] * d
            sums[0] += jnp.sum(d * moved[part][0], 0, keepdims=True)
            for offset in range(1, 4):
                sums[offset] += jnp.sum(d * moved[part][offset], 0, keepdims=True)
                marked = d * marks[offset - 1]
                joined = jnp.concatenate([marked, after[offset - 1, :, cols]], 0)
                after[offset - 1, :, cols] = marked[:8]
                up = pltpu.roll(joined, C + 8 - offset, 0)[:C]
                total = total + taps[offset : offset + 1, cols] * up
            back[rows, cols] = total.astype(BF16)
    for part in range(6):
        for offset in range(4):
            taps_grad[offset : offset + 1, part * 128 : part * 128 + 128] += taps_sum[part][offset]


def mix_backward(place, three, weights, raw, taps, aux, segs, saved, mm=fine):
    chunks, steps = 2, 4
    block = pl.BlockSpec((2, chunks, C, C), lambda i, place: (0, steps - 1 - i, 0, 0))
    rows = lambda width: pl.BlockSpec((1024, width), lambda i, place: (0, 0))
    return pl.pallas_call(
        functools.partial(backward_kernel, chunks, mm),
        grid_spec=pltpu.PrefetchScalarGridSpec(
            num_scalar_prefetch=1,
            grid=(steps,),
            in_specs=[pl.BlockSpec(part.shape, lambda i, place: (0, 0)) for part in three]
            + [pl.BlockSpec((D, 128), lambda i, place, n=n: (0, 7 + n)) for n in range(2)]
            + [
                rows(896),
                pl.BlockSpec((4, 768), lambda i, place: (0, 0)),
                pl.BlockSpec((chunks * C, 128), lambda i, place: (steps - 1 - i, 0)),
                pl.BlockSpec((1, chunks, 128), lambda i, place: (steps - 1 - i, 0, 0)),
            ]
            + [block] * 5,
            out_specs=[rows(896), pl.BlockSpec((4, 768), lambda i, place: (0, 0))],
            scratch_shapes=[
                pltpu.VMEM((3, 8, 768), F32),
                pltpu.VMEM((2, C, C), F32),
                pltpu.VMEM((1024, 256), F32),
            ],
        ),
        out_shape=[jax.ShapeDtypeStruct((1024, 896), BF16), jax.ShapeDtypeStruct((4, 768), F32)],
        compiler_params=pltpu.CompilerParams(vmem_limit_bytes=60 * 1024 * 1024),
        cost_estimate=pl.CostEstimate(flops=25 << 30, bytes_accessed=20 << 20, transcendentals=0),
        name="mix_backward",
    )(place, *three, weights, weights, raw, taps, aux, segs.reshape(steps, chunks, 128), *saved)


def marks_kernel(pack, aux, rows):
    segs = pack[:, 784:792].astype(F32)
    rows[...] = segs.T
    aux[...] = jnp.zeros_like(aux)
    for c in range(8):
        now = jnp.broadcast_to(segs[:, c : c + 1], (C, C))
        prior = jnp.broadcast_to(segs[:, c - 1 : c], (C, C)) if c else jnp.full((C, C), -1.0, F32)
        joined = jnp.concatenate([prior[120:], now], 0)
        columns = [pltpu.roll(joined, offset, 0)[8:] == now for offset in range(1, 4)]
        columns += [now == prior[C - 1 : C], now == now[C - 1 : C]]
        here = pl.ds(c * C, C)
        for n, column in enumerate(columns):
            aux[here, n : n + 1] = jnp.where(column, 1.0, 0.0)[:, :1]
        aux[here, 5:6] = now[:, :1]


AXES = ("yh", "x", "c", "z", "yl")
TEAM = ("z", "c")
RING = ("yh", "yl", "x")
PAD = 768
HID = 704
FORTH = [(a * 4 + x) * 2 + p for a in range(2) for p in range(2) for x in range(4)]
HOME = [(a * 2 + p) * 4 + x for a in range(2) for x in range(4) for p in range(2)]


def trade(value):
    return lax.ppermute(value, ("c", "yl"), [(0, 0), (1, 2), (2, 1), (3, 3)])


def mate(value):
    return lax.ppermute(value, "c", [(0, 1), (1, 0)])


def ahead(value):
    return lax.ppermute(value, "z", [(n, (n + 1) % 4) for n in range(4)])


def behind(value):
    return lax.ppermute(value, "z", [(n, (n - 1) % 4) for n in range(4)])


def local_call(kernel, name, outs, *operands, waits=(), limit=48):
    count = len(operands)

    def body(*refs):
        kernel(*refs[:count], *refs[count + len(waits) :])

    def whole(shape):
        return pl.BlockSpec(shape, lambda i: (0,) * len(shape))

    return pl.pallas_call(
        body,
        grid=(1,),
        in_specs=[whole(part.shape) for part in operands] + [pl.BlockSpec(memory_space=pl.ANY)] * len(waits),
        out_specs=[whole(shape) for shape, _ in outs],
        out_shape=[jax.ShapeDtypeStruct(shape, kind) for shape, kind in outs],
        compiler_params=pltpu.CompilerParams(vmem_limit_bytes=limit * 1024 * 1024),
        name=name,
    )(*operands, *waits)


def inverse_rms(rows):
    return lax.rsqrt(jnp.mean(rows * rows, -1, keepdims=True) + EPS)


def norm_back(normed, scale, scaled):
    return scale * (scaled - normed * jnp.mean(scaled * normed, -1, keepdims=True))


def put(out, value, blocks, at=0):
    for n, block in enumerate(blocks):
        out[:, at + n * 128 : at + n * 128 + 128] = value[:, block * 128 : block * 128 + 128].astype(out.dtype)


def norm_kernel(pack, rows, out):
    value = pack[:, 1152:].astype(F32)
    put(rows, value, FORTH)
    put(out, value * inverse_rms(value), FORTH)


def order_kernel(rows, out):
    put(out, rows[...], FORTH)


def ends_kernel(before, after, high, low):
    high[...] = before[:64]
    low[...] = after[64:]


def turn_kernel(*refs):
    at = 0
    for ref in refs[:2]:
        refs[-1][:, at : at + ref.shape[0]] = ref[...].T
        at += ref.shape[0]


def turned(parts, wait):
    block = 512
    return pl.pallas_call(
        turn_kernel,
        grid=(D // block,),
        in_specs=[pl.BlockSpec((part.shape[0], block), lambda i: (0, i)) for part in parts]
        + [pl.BlockSpec(memory_space=pl.ANY)],
        out_specs=pl.BlockSpec((block, 1024), lambda i: (i, 0)),
        out_shape=jax.ShapeDtypeStruct((D, 1024), BF16),
        compiler_params=pltpu.CompilerParams(vmem_limit_bytes=60 * 1024 * 1024),
        name="turned",
    )(*parts, wait)


def landed(own, up_high, up_low, down_high, down_low):
    high = up_high[...].astype(F32) + down_high[...].astype(F32)
    low = up_low[...].astype(F32) + down_low[...].astype(F32)
    return own[...] + jnp.concatenate([high, low], 0)


def middle_kernel(rows, own, up_high, up_low, down_high, down_low, middle, normed):
    value = rows[...].astype(F32) + landed(own, up_high, up_low, down_high, down_low)
    middle[...] = value
    normed[...] = (value * inverse_rms(value)).astype(BF16)


def second_kernel(middle, grad, scaled, out, low):
    value = middle[...]
    scale = inverse_rms(value)
    total = grad[...].astype(F32) + norm_back(value * scale, scale, scaled[...].astype(F32))
    out[...] = total
    low[...] = total.astype(BF16)


def first_kernel(rows, grad, own, up_high, up_low, down_high, down_low, out):
    value = rows[...].astype(F32)
    scale = inverse_rms(value)
    scaled = landed(own, up_high, up_low, down_high, down_low)
    put(out, grad[...] + norm_back(value * scale, scale, scaled), HOME)


def result_kernel(middle, own, up_high, up_low, down_high, down_low, out):
    put(out, middle[...] + landed(own, up_high, up_low, down_high, down_low), HOME)


def mix_pack_kernel(query, key, value, beta, taps, segs, out_w, gain_one, gain_two, tokens, out, gains):
    for n, ref in enumerate((query, key, value)):
        for h in range(2):
            out[:, h * 384 + n * 128 : h * 384 + n * 128 + 128] = ref[:, h * 128 : h * 128 + 128]
    out[:, 768:896] = jnp.zeros((128, 128), BF16)
    out[:, 768:776] = jnp.concatenate([beta[...].astype(F32), jnp.zeros((6, 128), F32)], 0).T.astype(BF16)
    out[:24, 776:784] = taps[...]
    out[:, 784:792] = segs[...].astype(F32).T.astype(BF16)
    out[:, 896:1152] = out_w[...].astype(F32).T.astype(BF16)
    gains[...] = jnp.concatenate([gain_one[...], gain_two[...]], 0)
    out[:, 1152:] = tokens[...]


def mix_scale_kernel(pack, gain, out):
    out[:, :768] = (pack[:, :768].astype(F32) * gain[...]).astype(BF16)
    small = pack[:, 768:896].astype(F32)
    lane = lax.broadcasted_iota(jnp.int32, small.shape, 1)
    out[:, 768:896] = jnp.where(lane < 2, small * gain[...], small).astype(BF16)
    out[:, 896:] = pack[:, 896:1152]


def ffn_pack_kernel(gate, up, down, out):
    for n, ref in enumerate((gate, up, down)):
        for j in range(3):
            count = min(256, HID - 256 * j)
            at = 768 * j + 256 * n
            out[:, at : at + count] = ref[256 * j : 256 * j + count, :].astype(F32).T.astype(BF16)
            if count < 256:
                out[:, at + count : at + 256] = jnp.zeros((128, 256 - count), BF16)


def ffn_scale_kernel(pack, gain, out):
    for j in range(3):
        at = 768 * j
        out[:, at : at + 512] = (pack[:, at : at + 512].astype(F32) * gain[...]).astype(BF16)
        out[:, at + 512 : at + 768] = pack[:, at + 512 : at + 768]


def ffn_sums_kernel(grads, weights, out, copy):
    copy[...] = grads[...]
    total = jnp.zeros((128, 1), F32)
    for j in range(3):
        here = slice(768 * j, 768 * j + 512)
        total = total + jnp.sum(grads[:, here].astype(F32) * weights[:, here].astype(F32), 1, keepdims=True)
    out[...] = total.reshape(1, 128)


def ffn_unpack_kernel(pack, gain, gate, up, down):
    for n, ref in enumerate((gate, up, down)):
        for j in range(3):
            count = min(256, HID - 256 * j)
            at = 768 * j + 256 * n
            value = pack[:, at : at + 256].astype(F32).T[:count]
            ref[256 * j : 256 * j + count, :] = value if n == 2 else value * gain[...]


def mix_unpack_kernel(pack, gain, query, key, value, beta, taps, out):
    for h in range(2):
        for n, ref in enumerate((query, key, value)):
            at = 384 * h + 128 * n
            ref[:, h * 128 : h * 128 + 128] = pack[at : at + 128, :].astype(F32) * gain[...]
    beta[...] = pack[768:770, :].astype(F32) * gain[...].reshape(1, 128)
    taps[...] = pack[770:772, :].astype(F32)
    out[...] = pack[784:, :].astype(F32)


def cross_kernel(same, other, own, up, down, after_high, after_low, before_high, before_low):
    total = same[...].astype(F32) + other[...].astype(F32)
    own[...] = total[:128]
    after_high[...] = total[128:192]
    after_low[...] = total[192:256].astype(BF16)
    before_high[...] = total[256:320].astype(BF16)
    before_low[...] = total[320:384]
    up[...] = total[384:448].astype(BF16)
    down[...] = total[448:].astype(BF16)


def pass_kernel(high, up, low, down, after, before):
    after[...] = (high[...] + up[...].astype(F32)).astype(BF16)
    before[...] = (low[...] + down[...].astype(F32)).astype(BF16)


def join_kernel(*refs):
    refs[-1][...] = jnp.concatenate([ref[...] for ref in refs[:-1]], 0)


def join(*parts):
    count = sum(part.shape[0] for part in parts)
    return local_call(join_kernel, "join", [((count, parts[0].shape[1]), BF16)], *parts)[0]


def gather_team(rows):
    before, after = ahead(rows), behind(rows)
    high, low = local_call(ends_kernel, "ends", [((64, D), BF16)] * 2, before, after)
    same = join(rows, after, before, ahead(high), behind(low))
    return same, mate(same)


def sum_team(same, other, waits=()):
    own, up, down, after_high, after_low, before_high, before_low = local_call(
        cross_kernel,
        "cross",
        [((128, D), F32)] + [((64, D), kind) for kind in (BF16, BF16, F32, BF16, BF16, F32)],
        same,
        mate(other),
        waits=waits,
        limit=60,
    )
    up, down = ahead(up), behind(down)
    after_low, before_high = ahead(after_low), behind(before_high)
    passed, before_low = local_call(
        pass_kernel, "pass_sum", [((64, D), BF16)] * 2, after_high, up, before_low, down
    )
    return (own, ahead(passed), after_low, before_high, behind(before_low)), passed


def gather_rows(rows):
    return lax.all_gather(rows, TEAM, axis=0, tiled=True)


def sum_rows(part):
    return lax.psum_scatter(part, TEAM, scatter_dimension=0, tiled=True)


def gather_ring(rows):
    return lax.all_gather(rows, RING, axis=0, tiled=True)


def swap_ring(part):
    return lax.all_to_all(part, RING, 0, 0, tiled=True)


def total_kernel(parts, pack, out, sums):
    total = parts[0].astype(F32)
    for n in range(1, 16):
        total = total + parts[n].astype(F32)
    out[...] = total.astype(BF16)
    small = pack[:, 768:896].astype(F32).T
    across = jnp.sum(total[768:770, :] * small[:2], 0, keepdims=True)
    rows = jnp.zeros((128, 1), F32)
    for n in range(6):
        here = slice(128 * n, 128 * n + 128)
        rows = rows + jnp.sum(total[here, :] * pack[:, here].astype(F32), 1, keepdims=True)
    sums[...] = across + rows.reshape(1, 128)


def matmul(left, right, dims, kind=F32):
    return lax.dot_general(left, right, dims, preferred_element_type=F32).astype(kind)


def ffn_kernel(source, *refs):
    parts, grads, (weights, active, back, second, total) = refs[:2], refs[2:4], refs[4:]
    step = pl.program_id(0)
    row = 0
    for part, grad in zip(parts, grads):
        count = part.shape[0]
        here = slice(row, row + count)
        both = dot(part[...], weights[:, :512], NN)
        grad_active = dot(grad[...], weights[:, 512:], NN)
        gate, up = both[:, :256], both[:, 256:]
        sigma = sigmoid(gate)
        swish = gate * sigma
        active[here, :] = (swish * up).astype(BF16)
        slope = sigma * (1.0 + gate * (1.0 - sigma))
        backs = jnp.concatenate([grad_active * up * slope, grad_active * swish], 1).astype(BF16)
        back[here, :] = backs
        piece = dot(backs, weights[:, :512], NT)

        @pl.when(step == 0)
        def _():
            total[here, :] = piece

        @pl.when(step == 1)
        def _():
            total[here, :] = total[here, :] + piece

        @pl.when(step == 2)
        def _():
            done = (total[here, :] + piece).astype(BF16)
            for n in range(count // C):
                second[spot(source, row // C + n), :] = done[n * C : n * C + C]

        row += count


def ffn(source, parts, grads, weights):
    whole = [pl.BlockSpec(part.shape, lambda j, source: (0, 0)) for part in parts]
    return pl.pallas_call(
        ffn_kernel,
        grid_spec=pltpu.PrefetchScalarGridSpec(
            num_scalar_prefetch=1,
            grid=(3,),
            in_specs=whole + whole + [pl.BlockSpec((D, 768), lambda j, source: (0, j))],
            out_specs=[
                pl.BlockSpec((1024, 256), lambda j, source: (0, j)),
                pl.BlockSpec((1024, 512), lambda j, source: (0, j)),
                pl.BlockSpec((1024, D), lambda j, source: (0, 0)),
            ],
            scratch_shapes=[pltpu.VMEM((1024, D), F32)],
        ),
        out_shape=[
            jax.ShapeDtypeStruct((1024, 768), BF16),
            jax.ShapeDtypeStruct((1024, 1536), BF16),
            jax.ShapeDtypeStruct((1024, D), BF16),
        ],
        compiler_params=pltpu.CompilerParams(vmem_limit_bytes=60 * 1024 * 1024),
        cost_estimate=pl.CostEstimate(flops=2 * 1024 * D * 1280 * 3, bytes_accessed=30 << 20, transcendentals=0),
        name="ffn",
    )(source, *parts, *grads, weights)


def ffn_grad_kernel(*refs):
    parts, grads, (back, active, out) = refs[:2], refs[2:4], refs[4:]
    seq = jnp.concatenate([ref[...].T for ref in parts], 1)
    dy = jnp.concatenate([ref[...].T for ref in grads], 1)
    for j in range(3):
        at = j * 768
        out[:, at : at + 512] = dot(seq, back[:, j * 512 : j * 512 + 512], NN).astype(BF16)
        out[:, at + 512 : at + 768] = dot(dy, active[:, j * 256 : j * 256 + 256], NN).astype(BF16)


def ffn_grad(parts, grads, back, active):
    block = 512
    return pl.pallas_call(
        ffn_grad_kernel,
        grid=(D // block,),
        in_specs=[pl.BlockSpec((part.shape[0], block), lambda i: (0, i)) for part in (*parts, *grads)]
        + [pl.BlockSpec(part.shape, lambda i: (0, 0)) for part in (back, active)],
        out_specs=pl.BlockSpec((block, 2304), lambda i: (i, 0)),
        out_shape=jax.ShapeDtypeStruct((D, 2304), BF16),
        compiler_params=pltpu.CompilerParams(vmem_limit_bytes=60 * 1024 * 1024),
        cost_estimate=pl.CostEstimate(flops=2 * 1024 * D * 2304, bytes_accessed=20 << 20, transcendentals=0),
        name="ffn_grad",
    )(*parts, *grads, back, active)


def in_grad_kernel(one, back, taps, near, other, mixed, out):
    total = dot(one[...], back[...], NN)
    outer = 0.0
    at = 0
    for ref in (near, other):
        outer = outer + dot(mixed[at : at + ref.shape[0], :].T, ref[...], NN)
        at += ref.shape[0]
    small = total[:, 768:].T
    for r in range(4):
        rows = slice(r * 128, r * 128 + 128)
        for n in range(6):
            out[r, n * 128 : n * 128 + 128, :] = total[rows, n * 128 : n * 128 + 128].astype(BF16)
        tail = jnp.concatenate([small[:2, rows], taps[r], jnp.zeros((12, 128), F32)], 0)
        out[r, 768:784, :] = tail.astype(BF16)
        out[r, 784:, :] = outer[:, rows].astype(BF16)


def in_grad(one, back, taps, three, mixed):
    block = 512
    return pl.pallas_call(
        in_grad_kernel,
        grid=(D // block,),
        in_specs=[
            pl.BlockSpec((block, 1024), lambda i: (i, 0)),
            pl.BlockSpec(back.shape, lambda i: (0, 0)),
            pl.BlockSpec((4, 2, 128), lambda i: (i, 0, 0)),
            *[pl.BlockSpec((part.shape[0], block), lambda i: (0, i)) for part in three],
            pl.BlockSpec(mixed.shape, lambda i: (0, 0)),
        ],
        out_specs=pl.BlockSpec((4, 1040, 128), lambda i: (i, 0, 0)),
        out_shape=jax.ShapeDtypeStruct((16, 1040, 128), BF16),
        compiler_params=pltpu.CompilerParams(vmem_limit_bytes=60 * 1024 * 1024),
        cost_estimate=pl.CostEstimate(flops=2 * 1024 * D * 1152, bytes_accessed=8 << 20, transcendentals=0),
        name="in_grad",
    )(one, back, taps, *three, mixed)


def first_kernel_parts(back, weights, *outs):
    at = 0
    for out in outs:
        count = out.shape[0]
        out[...] = dot(back[at : at + count, :], weights[...], NT).astype(BF16)
        at += count


def first_parts(back, weights):
    block = 512
    return pl.pallas_call(
        first_kernel_parts,
        grid=(D // block,),
        in_specs=[pl.BlockSpec((1024, 896), lambda i: (0, 0)), pl.BlockSpec((block, 896), lambda i: (i, 0))],
        out_specs=[pl.BlockSpec((count, block), lambda i: (0, i)) for count in PARTS],
        out_shape=[jax.ShapeDtypeStruct((count, D), BF16) for count in PARTS],
        compiler_params=pltpu.CompilerParams(vmem_limit_bytes=60 * 1024 * 1024),
        cost_estimate=pl.CostEstimate(flops=2 * 1024 * D * 896, bytes_accessed=8 << 20, transcendentals=0),
        name="first_parts",
    )(back, weights)


def down_kernel(active, first, second, third, wait, *outs):
    right = jnp.concatenate([first[...], second[...], third[...]], 1)
    at = 0
    for out in outs:
        out[...] = dot(active[at : at + out.shape[0], :], right, NT).astype(BF16)
        at += out.shape[0]


def down_product(active, weights, wait):
    block = 512
    return pl.pallas_call(
        down_kernel,
        grid=(D // block,),
        in_specs=[pl.BlockSpec((1024, PAD), lambda i: (0, 0))]
        + [pl.BlockSpec((block, 256), lambda i, j=j: (i, 3 * j + 2)) for j in range(3)]
        + [pl.BlockSpec(memory_space=pl.ANY)],
        out_specs=[pl.BlockSpec((count, block), lambda i: (0, i)) for count in PARTS],
        out_shape=[jax.ShapeDtypeStruct((count, D), BF16) for count in PARTS],
        compiler_params=pltpu.CompilerParams(vmem_limit_bytes=60 * 1024 * 1024),
        cost_estimate=pl.CostEstimate(flops=2 * 1024 * D * 768, bytes_accessed=8 << 20, transcendentals=0),
        name="down_product",
    )(active, weights, weights, weights, wait)


def team_total(values, pair):
    values = values.reshape(4, 2, 16)
    here = lax.axis_index(pair)
    mine = lax.dynamic_index_in_dim(values, here, 1, False)
    other = lax.dynamic_index_in_dim(values, 1 - here, 1, False)
    mine = mine + lax.ppermute(other, pair, [(0, 1), (1, 0)])
    place = lax.axis_index("z")

    def block(distance):
        return lax.dynamic_index_in_dim(mine, (place + distance) & 3, 0, False)

    total = block(0)
    for distance in range(1, 4):
        total = total + lax.ppermute(block(distance), "z", [(n, (n + distance) % 4) for n in range(4)])
    return total


def on_device(
    tokens,
    segments,
    cotangent,
    attn_gain,
    w_query,
    w_key,
    w_value,
    w_beta,
    conv_weight,
    w_out,
    ffn_gain,
    w_gate,
    w_up,
    w_down,
):
    core, z = lax.axis_index("c"), lax.axis_index("z")
    true = jnp.arange(8, dtype=jnp.int32)
    distance, other = (true // 2 - z) & 3, (true % 2) ^ core
    place = (jnp.where(distance > 1, 5 - distance, distance) + 4 * other).astype(jnp.int32)

    source = jnp.sum(jnp.where(place[:, None] == true[None, :], true[:, None], 0), 0).astype(jnp.int32)

    mix_pack, gains = local_call(
        mix_pack_kernel,
        "mix_pack",
        [((128, 1152 + D), BF16), ((2, 16), F32)],
        w_query,
        w_key,
        w_value,
        w_beta.T,
        conv_weight.reshape(24, 8),
        segments.reshape(8, 128),
        w_out,
        attn_gain.reshape(1, 16),
        ffn_gain.reshape(1, 16),
        tokens,
        limit=60,
    )
    mix_pack = trade(mix_pack)
    rows, one = local_call(norm_kernel, "norm_one", [((128, D), BF16)] * 2, mix_pack)
    (grad_rows,) = local_call(order_kernel, "order_grad", [((128, D), BF16)], cotangent, limit=60)
    grad_rows = trade(grad_rows)
    (ffn_pack,) = local_call(ffn_pack_kernel, "ffn_pack", [((128, 2304), BF16)], w_gate.T, w_up.T, w_down, limit=60)
    ffn_pack = trade(ffn_pack)

    gains = jnp.broadcast_to(jnp.concatenate([gains, mate(gains)], 0)[None], (8, 4, 16))
    gains = lax.all_to_all(gains, ("z", "yl"), 0, 0, tiled=True).transpose(1, 0, 2).reshape(4, 128)
    home = gains[:2]
    away = jnp.where(core == lax.axis_index("yl"), gains[:2], gains[2:])
    (scaled_pack,) = local_call(mix_scale_kernel, "mix_scale", [((128, 1152), BF16)], mix_pack, away[0][:, None])
    mix_w = gather_ring(scaled_pack)

    one = gather_team(one)
    grads = gather_team(grad_rows)
    (scaled_ffn,) = local_call(
        ffn_scale_kernel, "ffn_scale", [((128, 2304), BF16)], ffn_pack, away[1][:, None]
    )
    ffn_w = gather_ring(scaled_ffn)

    taps = mix_w[:, 768:896].reshape(2, 2, 4, 128, 128)[:, :, :, :24, 8:16].reshape(2, 2, 4, 3, 4, 2, 8)
    taps = taps.transpose(4, 5, 3, 0, 2, 1, 6).reshape(4, 768).astype(F32)
    marks, seg_rows = local_call(marks_kernel, "marks", [((1024, 128), F32), ((8, 128), F32)], mix_pack)
    mixed, raw, *saved = mix_forward(place, one, mix_w, taps, marks, seg_rows, (scaled_ffn, grads[1]))
    middle, two = local_call(
        middle_kernel, "middle", [((128, D), F32), ((128, D), BF16)], rows, *sum_team(*saved[:2])[0]
    )
    one_turned = turned(one, saved[0])
    two = gather_team(two)
    active, ffn_back, second = ffn(source, two, grads, ffn_w)
    ffn_grads = ffn_grad(two, grads, ffn_back, active)
    result = down_product(active, ffn_w, second)
    middle_grad, three = local_call(
        second_kernel,
        "second",
        [((128, D), F32), ((128, D), BF16)],
        middle,
        grad_rows,
        sum_rows(second),
        waits=(ffn_grads, one_turned, result[0]),
    )
    ring_grads = lax.psum_scatter(ffn_grads, RING, scatter_dimension=0, tiled=True)
    three = gather_team(three)
    back, taps_grad = mix_backward(place, three, mix_w, raw, taps, marks, seg_rows, saved[2:])
    taps_grad = taps_grad.reshape(4, 2, 3, 2, 4, 2, 8).transpose(3, 5, 4, 1, 2, 0, 6).reshape(16, 2, 96)
    taps_grad = jnp.pad(taps_grad, ((0, 0), (0, 0), (0, 32)))
    ring_parts = lax.all_to_all(in_grad(one_turned, back, taps_grad, three, mixed), RING, 0, 0, tiled=True)
    terms, _ = sum_team(*first_parts(back, mix_w))
    (tokens_grad,) = local_call(first_kernel, "first", [((128, D), BF16)], rows, middle_grad, *terms)
    terms, passed = sum_team(*result, waits=terms[:1])
    (output,) = local_call(result_kernel, "result", [((128, D), BF16)], middle, *terms)
    ffn_sum, ring_grads = local_call(
        ffn_sums_kernel,
        "ffn_sums",
        [((1, 128), F32), ((128, 2304), BF16)],
        ring_grads,
        scaled_ffn,
        waits=(passed, tokens_grad),
    )
    grad_gate, grad_up, grad_down = local_call(
        ffn_unpack_kernel, "ffn_unpack", [((HID, 128), F32)] * 3, trade(ring_grads), home[1][None]
    )
    mix_grad, sums = local_call(
        total_kernel,
        "ring_total",
        [((1040, 128), BF16), ((1, 128), F32)],
        ring_parts,
        scaled_pack,
        waits=(tokens_grad, ffn_sum),
    )
    tokens_grad = trade(tokens_grad).astype(F32)
    output = trade(output)
    grad_query, grad_key, grad_value, grad_beta, grad_taps, grad_out = local_call(
        mix_unpack_kernel,
        "mix_unpack",
        [((128, 256), F32)] * 3 + [((2, 128), F32), ((2, 128), F32), ((256, 128), F32)],
        trade(mix_grad),
        home[0][:, None],
    )
    grad_taps = grad_taps[:, :96].reshape(2, 3, 4, 8).transpose(1, 2, 0, 3)
    return (
        output,
        tokens_grad,
        trade(team_total(sums, "c")) / attn_gain,
        grad_query,
        grad_key,
        grad_value,
        grad_beta.T,
        grad_taps,
        grad_out,
        trade(team_total(ffn_sum, "c")) / ffn_gain,
        grad_gate.T,
        grad_up.T,
        grad_down,
    )


def solution(mesh):
    dp, tensor = ("yh", "x", "c"), ("z", "yl")
    every = dp + tensor
    split = jax.sharding.Mesh(mesh.devices.reshape(2, 4, 2, 4, 2), AXES)
    placed = (
        P(every, None),
        P(dp),
        P(every, None),
        P(every),
        P(dp, tensor),
        P(dp, tensor),
        P(dp, tensor),
        P(dp, tensor),
        P(None, None, tensor, dp),
        P(tensor, dp),
        P(every),
        P(dp, tensor),
        P(dp, tensor),
        P(tensor, dp),
    )
    return jax.shard_map(
        on_device,
        mesh=split,
        in_specs=placed,
        out_specs=(
            P(every, None),
            P(every, None),
            P(every),
            P(dp, tensor),
            P(dp, tensor),
            P(dp, tensor),
            P(dp, tensor),
            P(None, None, tensor, dp),
            P(tensor, dp),
            P(every),
            P(dp, tensor),
            P(dp, tensor),
            P(tensor, dp),
        ),
        check_vma=False,
    )
```

```python
import functools
import jax
import jax.numpy as jnp
from jax import lax
from jax.experimental import pallas as pl
from jax.experimental.pallas import tpu as pltpu
from jax.sharding import PartitionSpec as P

C = 128
D = 2048
PARTS = (512, 512)
EPS = 1e-06
F32 = jnp.float32
BF16 = jnp.bfloat16
NN = (((1,), (0,)), ((), ()))
NT = (((1,), (1,)), ((), ()))
TN = (((0,), (0,)), ((), ()))


def dot(left, right, dims):
    return lax.dot_general(left, right, dims, preferred_element_type=F32)


def halves(value):
    high = value.astype(BF16)
    return high, (value - high.astype(F32)).astype(BF16)


def fine(left, right, dims):
    left_high, left_low = halves(left)
    right_high, right_low = halves(right)
    (over,), (under,) = dims[0]
    first = dot(
        jnp.concatenate([left_high, left_low], over), jnp.concatenate([right_high, right_high], under), dims
    )
    return first + dot(left_high, right_low, dims)


def sigmoid(v):
    return 1.0 / (1.0 + jnp.exp(-v))


def masks():
    row = lax.broadcasted_iota(jnp.int32, (C, C), 0)
    col = lax.broadcasted_iota(jnp.int32, (C, C), 1)
    return row, col


def shifted(rows, before, offset):
    joined = jnp.concatenate([before, rows], 0)
    return pltpu.roll(joined, offset, 0)[8:]


def convolved(rows, before, taps, marks):
    total = taps[0] * rows
    moved = []
    for offset in range(1, 4):
        term = shifted(rows, before, offset) * marks[offset - 1]
        moved.append(term)
        total = total + taps[offset] * term
    return total, moved


def inverses(systems):
    row, col = masks()
    eye = jnp.where(row == col, 1.0, 0.0)
    solved = []
    near = (row == col + 1) & ((row & 1) == 1)
    solved = [eye - jnp.where(near, a, 0.0) for a in systems]
    for level in range(1, 7):
        odd = ((row >> level) & 1) == 1
        off = odd & ((row >> level) == (col >> level) + 1)
        parts = [fine(x, jnp.where(off, a, 0.0), NN) for x, a in zip(solved, systems)]
        solved = [x - fine(p, x, NN) for x, p in zip(solved, parts)]
    return solved


def taps_of(taps, part, h):
    return [taps[row : row + 1] for row in range(part * 8 + h, part * 8 + 8, 2)]


def place_of(member):
    return (member // 8 * 4 + member % 4) * 2 + member // 4 % 2


def gathered_taps(weights):
    lane = lax.broadcasted_iota(jnp.int32, (C, C), 0)
    target = lax.broadcasted_iota(jnp.int32, (C, C), 1)
    total = jnp.zeros((32, C), F32)
    for member in range(16):
        chosen = (lane >= 8) & (lane < 16) & (target == lane - 8 + place_of(member) * 8)
        piece = weights[member * C : member * C + 32, 768:]
        total = total + dot(piece, jnp.where(chosen, 1.0, 0.0).astype(BF16), NN)
    return total


def forward_kernel(chunks, mm, place, same, other, weights, out_w, out_w_next, aux, segs, wait, wait_next, mixed, raw, taps, part_same, part_other, t_out, u_out, s_out, m_out, q_out, before, state):
    step = pl.program_id(0)

    @pl.when(step == 0)
    def _():
        raw[:512, :] = dot(same[...], weights[...], NN)
        raw[512:, :] = dot(other[...], weights[...], NN)
        taps[...] = gathered_taps(weights)
        before[...] = jnp.zeros_like(before)
        state[...] = jnp.zeros_like(state)

    row, col = masks()
    eye = jnp.where(row == col, 1.0, 0.0)
    taps_now = taps[...]
    items = []
    for c in range(chunks):
        rows, fixed = spot(place, chunks * step + c), pl.ds(c * C, C)
        prev = before[...] if c == 0 else raw[spot(place, chunks * step + c - 1, 120, 8), :768]
        marks = [aux[fixed, j : j + 1] for j in range(3)]
        carried, closing, seg = aux[fixed, 3:4], aux[fixed, 4:5], aux[fixed, 5:6]
        same_doc = seg == segs[0, c : c + 1, :]
        gamma = carried[C - 1 : C]
        for h in range(2):
            acts = []
            for part in range(3):
                cols = slice(384 * h + 128 * part, 384 * h + 128 * part + 128)
                conv, _ = convolved(raw[rows, cols], prev[:, cols], taps_of(taps_now, part, h), marks)
                acts.append(conv * sigmoid(conv))
            q, k, v = acts
            q = q * lax.rsqrt(jnp.sum(q * q, -1, keepdims=True) + EPS)
            k = k * lax.rsqrt(jnp.sum(k * k, -1, keepdims=True) + EPS)
            b = sigmoid(raw[rows, 768 + h : 769 + h])
            items.append((q, k, v, b, carried, closing, same_doc, gamma))
    before[...] = raw[spot(place, chunks * step + chunks - 1, 120, 8), :768]
    systems, scores = [], []
    for q, k, v, b, carried, closing, same_doc, gamma in items:
        gram = mm(k, k, NT)
        systems.append(jnp.where(same_doc & (row > col), b * gram, 0.0))
        scores.append(jnp.where(same_doc & (row >= col), mm(q, k, NT), 0.0))
    solved = inverses(systems)
    wus = [
        mm(t, jnp.concatenate([(i[4] * i[3]) * i[1], i[3] * i[2]], 1), NN)
        for t, i in zip(solved, items)
    ]
    mns = [mm(i[5] * i[1], wu, TN) for wu, i in zip(wus, items)]
    qos = [mm(p, wu, NN) for p, wu in zip(scores, wus)]
    for n, i in enumerate(items):
        c, h = n // 2, n % 2
        t_out[h, c] = solved[n]
        now = state[h]
        s_out[h, c] = now
        move = i[7] * eye - mns[n][:, :128]
        query = i[4] * i[0] - qos[n][:, :128]
        m_out[h, c] = move
        q_out[h, c] = query
        state[h] = mm(move, now, NN) + mns[n][:, 128:]
        u_out[h, c] = wus[n][:, 128:] - mm(wus[n][:, :128], now, NN)
        result = (mm(query, now, NN) + qos[n][:, 128:]).astype(BF16)
        mixed[spot(place, chunks * step + c), h * 128 : h * 128 + 128] = result

    @pl.when(step == pl.num_programs(0) - 1)
    def _():
        project = jnp.concatenate([out_w[...], out_w_next[...]], 1)
        at = 0
        for ref in (part_same, part_other):
            count = ref.shape[0]
            ref[...] = dot(mixed[at : at + count, :], project, NT).astype(BF16)
            at += count


def spot(place, block, start=0, count=C):
    return pl.ds(pl.multiple_of(place[block] * C + start, 8), count)


def mix_forward(place, parts, weights, aux, segs, waits, mm=fine):
    chunks, steps = 4, 2
    saved = jax.ShapeDtypeStruct((2, 8, C, C), F32)
    block = pl.BlockSpec((2, chunks, C, C), lambda i, place: (0, i, 0, 0))
    rows = lambda width: pl.BlockSpec((1024, width), lambda i, place: (0, 0))
    return pl.pallas_call(
        functools.partial(forward_kernel, chunks, mm),
        grid_spec=pltpu.PrefetchScalarGridSpec(
            num_scalar_prefetch=1,
            grid=(steps,),
            in_specs=[
                *[pl.BlockSpec((part.shape[0], D), lambda i, place: (0, 0)) for part in parts],
                pl.BlockSpec((D, 896), lambda i, place: (0, 0)),
                *[pl.BlockSpec((D, 128), lambda i, place, n=n: (0, 7 + n)) for n in range(2)],
                pl.BlockSpec((chunks * C, 128), lambda i, place: (i, 0)),
                pl.BlockSpec((1, chunks, 128), lambda i, place: (i, 0, 0)),
                *[pl.BlockSpec(memory_space=pl.ANY) for _ in waits],
            ],
            out_specs=[rows(256), rows(896), pl.BlockSpec((32, C), lambda i, place: (0, 0))]
            + [pl.BlockSpec((count, D), lambda i, place: (0, 0)) for count in PARTS]
            + [block] * 5,
            scratch_shapes=[pltpu.VMEM((8, 768), F32), pltpu.VMEM((2, C, C), F32)],
        ),
        out_shape=[jax.ShapeDtypeStruct((1024, 256), BF16)]
        + [jax.ShapeDtypeStruct((1024, 896), F32), jax.ShapeDtypeStruct((32, C), F32)]
        + [jax.ShapeDtypeStruct((count, D), BF16) for count in PARTS]
        + [saved] * 5,
        compiler_params=pltpu.CompilerParams(vmem_limit_bytes=48 * 1024 * 1024),
        cost_estimate=pl.CostEstimate(flops=20 << 30, bytes_accessed=20 << 20, transcendentals=0),
        name="mix_forward",
    )(place, *parts, weights, weights, weights, aux, segs.reshape(steps, chunks, 128), *waits)


def backward_kernel(chunks, mm, place, near, other, out_w, out_w_next, raw, taps, aux, segs, t_in, u_in, s_in, m_in, q_in, back, taps_grad, after, adjoint, grad):
    step = pl.program_id(0)
    last = pl.num_programs(0) - 1
    start = chunks * (last - step)

    @pl.when(step == 0)
    def _():
        weights = jnp.concatenate([out_w[...], out_w_next[...]], 1)
        at = 0
        for ref in (near, other):
            grad[at : at + ref.shape[0], :] = dot(ref[...], weights, NN)
            at += ref.shape[0]
        after[...] = jnp.zeros_like(after)
        adjoint[...] = jnp.zeros_like(adjoint)
        taps_grad[...] = jnp.zeros_like(taps_grad)
        back[:, 768:] = jnp.zeros_like(back[:, 768:])

    row, col = masks()
    taps_now = taps[...]
    taps_sum = [[jnp.zeros((1, 128), F32) for _ in range(4)] for _ in range(6)]
    items = []
    for c in range(chunks):
        rows, fixed = spot(place, start + c), pl.ds(c * C, C)
        if c == 0:
            prev = jnp.where(step == last, 0.0, raw[spot(place, jnp.maximum(start - 1, 0), 120, 8), :768])
        else:
            prev = raw[spot(place, start + c - 1, 120, 8), :768]
        marks = [aux[fixed, j : j + 1] for j in range(3)]
        carried, closing, seg = aux[fixed, 3:4], aux[fixed, 4:5], aux[fixed, 5:6]
        same = seg == segs[0, c : c + 1, :]
        for h in range(2):
            acts, slopes, moved = [], [], []
            for part in range(3):
                cols = slice(384 * h + 128 * part, 384 * h + 128 * part + 128)
                now = raw[rows, cols]
                conv, terms = convolved(now, prev[:, cols], taps_of(taps_now, part, h), marks)
                s = sigmoid(conv)
                acts.append(conv * s)
                slopes.append(s * (1.0 + conv * (1.0 - s)))
                moved.append([now] + terms)
            q, k, v = acts
            rq = lax.rsqrt(jnp.sum(q * q, -1, keepdims=True) + EPS)
            rk = lax.rsqrt(jnp.sum(k * k, -1, keepdims=True) + EPS)
            b = sigmoid(raw[rows, 768 + h : 769 + h])
            do = grad[rows, 128 * h : 128 * h + 128]
            items.append((c, h, marks, carried, closing, same, slopes, moved, q * rq, k * rk, v, b, rq, rk, do))
    for item in sorted(items, key=lambda item: (-item[0], item[1])):
        c, h, marks, carried, closing, same, slopes, moved, q, k, v, b, rq, rk, do = item
        t, u, s, m, qe = t_in[h, c], u_in[h, c], s_in[h, c], m_in[h, c], q_in[h, c]
        g = adjoint[h]
        adjoint[h] = mm(m, g, TN) + mm(qe, do, TN)
        gram = mm(k, k, NT)
        score = jnp.where(same & (row >= col), mm(q, k, NT), 0.0)
        du = mm(score, do, TN) + mm(closing * k, g, NN)
        dr = mm(t, du, TN)
        dps = mm(jnp.concatenate([do, dr], 0), u, NT)
        dp = jnp.where(same & (row >= col), dps[:C], 0.0)
        da = jnp.where(same & (row > col), -dps[C:], 0.0)
        e = b * da
        sides = mm(jnp.concatenate([carried * do, (carried * b) * dr], 0), s, NT)
        inner = mm(jnp.concatenate([dp, e], 0), k, NN)
        dq = sides[:C] + inner[:C]
        dk = (
            inner[C:]
            - sides[C:]
            + mm(jnp.concatenate([dp, e], 0), jnp.concatenate([q, k], 0), TN)
            + closing * mm(u, g, NT)
        )
        ks = mm(k, s, NN)
        db = jnp.sum(dr * (v - carried * ks) + da * gram, -1, keepdims=True)
        backs = (
            rq * (dq - q * jnp.sum(dq * q, -1, keepdims=True)),
            rk * (dk - k * jnp.sum(dk * k, -1, keepdims=True)),
            b * dr,
        )
        rows = spot(place, start + c)
        back[rows, 768 + h : 769 + h] = (db * b * (1.0 - b)).astype(BF16)
        for part in range(3):
            d = backs[part] * slopes[part]
            cols = slice(384 * h + part * 128, 384 * h + part * 128 + 128)
            sums = taps_sum[3 * h + part]
            taps_here = taps_of(taps_now, part, h)
            total = taps_here[0] * d
            sums[0] += jnp.sum(d * moved[part][0], 0, keepdims=True)
            for offset in range(1, 4):
                sums[offset] += jnp.sum(d * moved[part][offset], 0, keepdims=True)
                marked = d * marks[offset - 1]
                joined = jnp.concatenate([marked, after[offset - 1, :, cols]], 0)
                after[offset - 1, :, cols] = marked[:8]
                up = pltpu.roll(joined, C + 8 - offset, 0)[:C]
                total = total + taps_here[offset] * up
            back[rows, cols] = total.astype(BF16)
    for n in range(6):
        for offset in range(4):
            at = (n % 3 * 4 + offset) * 2 + n // 3
            taps_grad[at : at + 1, :] += taps_sum[n][offset]


def mix_backward(place, three, weights, raw, taps, aux, segs, saved, mm=fine):
    chunks, steps = 2, 4
    block = pl.BlockSpec((2, chunks, C, C), lambda i, place: (0, steps - 1 - i, 0, 0))
    rows = lambda width: pl.BlockSpec((1024, width), lambda i, place: (0, 0))
    return pl.pallas_call(
        functools.partial(backward_kernel, chunks, mm),
        grid_spec=pltpu.PrefetchScalarGridSpec(
            num_scalar_prefetch=1,
            grid=(steps,),
            in_specs=[pl.BlockSpec(part.shape, lambda i, place: (0, 0)) for part in three]
            + [pl.BlockSpec((D, 128), lambda i, place, n=n: (0, 7 + n)) for n in range(2)]
            + [
                rows(896),
                pl.BlockSpec((32, C), lambda i, place: (0, 0)),
                pl.BlockSpec((chunks * C, 128), lambda i, place: (steps - 1 - i, 0)),
                pl.BlockSpec((1, chunks, 128), lambda i, place: (steps - 1 - i, 0, 0)),
            ]
            + [block] * 5,
            out_specs=[rows(896), pl.BlockSpec((32, C), lambda i, place: (0, 0))],
            scratch_shapes=[
                pltpu.VMEM((3, 8, 768), F32),
                pltpu.VMEM((2, C, C), F32),
                pltpu.VMEM((1024, 256), F32),
            ],
        ),
        out_shape=[jax.ShapeDtypeStruct((1024, 896), BF16), jax.ShapeDtypeStruct((32, C), F32)],
        compiler_params=pltpu.CompilerParams(vmem_limit_bytes=60 * 1024 * 1024),
        cost_estimate=pl.CostEstimate(flops=25 << 30, bytes_accessed=20 << 20, transcendentals=0),
        name="mix_backward",
    )(place, *three, weights, weights, raw, taps, aux, segs.reshape(steps, chunks, 128), *saved)


def marks_kernel(pack, aux, rows):
    segs = pack[:, 784:792].astype(F32)
    rows[...] = segs.T
    aux[...] = jnp.zeros_like(aux)
    for c in range(8):
        now = jnp.broadcast_to(segs[:, c : c + 1], (C, C))
        prior = jnp.broadcast_to(segs[:, c - 1 : c], (C, C)) if c else jnp.full((C, C), -1.0, F32)
        joined = jnp.concatenate([prior[120:], now], 0)
        columns = [pltpu.roll(joined, offset, 0)[8:] == now for offset in range(1, 4)]
        columns += [now == prior[C - 1 : C], now == now[C - 1 : C]]
        here = pl.ds(c * C, C)
        for n, column in enumerate(columns):
            aux[here, n : n + 1] = jnp.where(column, 1.0, 0.0)[:, :1]
        aux[here, 5:6] = now[:, :1]


AXES = ("yh", "x", "c", "z", "yl")
TEAM = ("z", "c")
RING = ("yh", "yl", "x")
PAD = 768
HID = 704
FORTH = [(a * 4 + x) * 2 + p for a in range(2) for p in range(2) for x in range(4)]
HOME = [(a * 2 + p) * 4 + x for a in range(2) for x in range(4) for p in range(2)]


def trade(value):
    return lax.ppermute(value, ("c", "yl"), [(0, 0), (1, 2), (2, 1), (3, 3)])


def mate(value):
    return lax.ppermute(value, "c", [(0, 1), (1, 0)])


def ahead(value):
    return lax.ppermute(value, "z", [(n, (n + 1) % 4) for n in range(4)])


def behind(value):
    return lax.ppermute(value, "z", [(n, (n - 1) % 4) for n in range(4)])


def local_call(kernel, name, outs, *operands, waits=(), limit=48):
    count = len(operands)

    def body(*refs):
        kernel(*refs[:count], *refs[count + len(waits) :])

    def whole(shape):
        return pl.BlockSpec(shape, lambda i: (0,) * len(shape))

    return pl.pallas_call(
        body,
        grid=(1,),
        in_specs=[whole(part.shape) for part in operands] + [pl.BlockSpec(memory_space=pl.ANY)] * len(waits),
        out_specs=[whole(shape) for shape, _ in outs],
        out_shape=[jax.ShapeDtypeStruct(shape, kind) for shape, kind in outs],
        compiler_params=pltpu.CompilerParams(vmem_limit_bytes=limit * 1024 * 1024),
        name=name,
    )(*operands, *waits)


def inverse_rms(rows):
    return lax.rsqrt(jnp.mean(rows * rows, -1, keepdims=True) + EPS)


def norm_back(normed, scale, scaled):
    return scale * (scaled - normed * jnp.mean(scaled * normed, -1, keepdims=True))


def put(out, value, blocks, at=0):
    for n, block in enumerate(blocks):
        out[:, at + n * 128 : at + n * 128 + 128] = value[:, block * 128 : block * 128 + 128].astype(out.dtype)


def norm_kernel(pack, rows, out):
    value = pack[:, 1152:].astype(F32)
    put(rows, value, FORTH)
    put(out, value * inverse_rms(value), FORTH)


def order_kernel(rows, out):
    put(out, rows[...], FORTH)


def ends_kernel(before, after, high, low):
    high[...] = before[:64]
    low[...] = after[64:]


def turn_kernel(*refs):
    at = 0
    for ref in refs[:2]:
        refs[-1][:, at : at + ref.shape[0]] = ref[...].T
        at += ref.shape[0]


def turned(parts, wait):
    block = 512
    return pl.pallas_call(
        turn_kernel,
        grid=(D // block,),
        in_specs=[pl.BlockSpec((part.shape[0], block), lambda i: (0, i)) for part in parts]
        + [pl.BlockSpec(memory_space=pl.ANY)],
        out_specs=pl.BlockSpec((block, 1024), lambda i: (i, 0)),
        out_shape=jax.ShapeDtypeStruct((D, 1024), BF16),
        compiler_params=pltpu.CompilerParams(vmem_limit_bytes=60 * 1024 * 1024),
        name="turned",
    )(*parts, wait)


def landed(own, up_high, up_low, down_high, down_low):
    high = up_high[...].astype(F32) + down_high[...].astype(F32)
    low = up_low[...].astype(F32) + down_low[...].astype(F32)
    return own[...] + jnp.concatenate([high, low], 0)


def middle_kernel(rows, own, up_high, up_low, down_high, down_low, middle, normed):
    value = rows[...].astype(F32) + landed(own, up_high, up_low, down_high, down_low)
    middle[...] = value
    normed[...] = (value * inverse_rms(value)).astype(BF16)


def second_kernel(middle, grad, scaled, out, low):
    value = middle[...]
    scale = inverse_rms(value)
    total = grad[...].astype(F32) + norm_back(value * scale, scale, scaled[...].astype(F32))
    out[...] = total
    low[...] = total.astype(BF16)


def first_kernel(rows, grad, own, up_high, up_low, down_high, down_low, out):
    value = rows[...].astype(F32)
    scale = inverse_rms(value)
    scaled = landed(own, up_high, up_low, down_high, down_low)
    put(out, grad[...] + norm_back(value * scale, scale, scaled), HOME)


def widen_kernel(rows, out):
    out[...] = rows[...].astype(F32)


def result_kernel(middle, own, up_high, up_low, down_high, down_low, out):
    put(out, middle[...] + landed(own, up_high, up_low, down_high, down_low), HOME)


def mix_pack_kernel(query, key, value, beta, taps, segs, out_w, gain_one, gain_two, tokens, out, gains):
    for n, ref in enumerate((query, key, value)):
        for h in range(2):
            out[:, h * 384 + n * 128 : h * 384 + n * 128 + 128] = ref[:, h * 128 : h * 128 + 128]
    out[:, 768:896] = jnp.zeros((128, 128), BF16)
    out[:, 768:776] = jnp.concatenate([beta[...].astype(F32), jnp.zeros((6, 128), F32)], 0).T.astype(BF16)
    out[:24, 776:784] = taps[...]
    out[:, 784:792] = segs[...].astype(F32).T.astype(BF16)
    out[:, 896:1152] = out_w[...].astype(F32).T.astype(BF16)
    for n in range(16):
        gains[n] = jnp.concatenate([gain_one[...], gain_two[...]], 0)
    out[:, 1152:] = tokens[...]


def mix_scale_kernel(pack, gain, out):
    out[:, :768] = (pack[:, :768].astype(F32) * gain[...]).astype(BF16)
    small = pack[:, 768:896].astype(F32)
    lane = lax.broadcasted_iota(jnp.int32, small.shape, 1)
    out[:, 768:896] = jnp.where(lane < 2, small * gain[...], small).astype(BF16)
    out[:, 896:] = pack[:, 896:1152]


def ffn_pack_kernel(gate, up, down, out):
    for n, ref in enumerate((gate, up, down)):
        for j in range(3):
            count = min(256, HID - 256 * j)
            at = 768 * j + 256 * n
            out[:, at : at + count] = ref[256 * j : 256 * j + count, :].astype(F32).T.astype(BF16)
            if count < 256:
                out[:, at + count : at + 256] = jnp.zeros((128, 256 - count), BF16)


def ffn_scale_kernel(pack, gain, out):
    for j in range(3):
        at = 768 * j
        out[:, at : at + 512] = (pack[:, at : at + 512].astype(F32) * gain[...]).astype(BF16)
        out[:, at + 512 : at + 768] = pack[:, at + 512 : at + 768]


def ffn_unpack_kernel(pack, gain, gate, up, down):
    for n, ref in enumerate((gate, up, down)):
        for block in range(6):
            count = min(128, HID - 128 * block)
            at = 1040 + 768 * (block // 2) + 256 * n + 128 * (block % 2)
            value = pack[at : at + 128, :].astype(F32).T[:count]
            ref[128 * block : 128 * block + count, :] = value if n == 2 else value * gain[...]


def mix_unpack_kernel(pack, gain, query, key, value, beta, taps, out):
    for h in range(2):
        for n, ref in enumerate((query, key, value)):
            at = 384 * h + 128 * n
            ref[:, h * 128 : h * 128 + 128] = pack[at : at + 128, :].astype(F32) * gain[...]
    beta[...] = pack[768:784, :].astype(F32)[:2] * gain[...].reshape(1, 128)
    taps[...] = pack[768:784, :].astype(F32)[2:10]
    out[...] = pack[784:1040, :].astype(F32)


def cross_kernel(same, other, own, up, down, after_high, after_low, before_high, before_low):
    total = same[...].astype(F32) + other[...].astype(F32)
    own[...] = total[:128]
    after_high[...] = total[128:192]
    after_low[...] = total[192:256].astype(BF16)
    before_high[...] = total[256:320].astype(BF16)
    before_low[...] = total[320:384]
    up[...] = total[384:448].astype(BF16)
    down[...] = total[448:].astype(BF16)


def pass_kernel(high, up, low, down, after, before):
    after[...] = (high[...] + up[...].astype(F32)).astype(BF16)
    before[...] = (low[...] + down[...].astype(F32)).astype(BF16)


def join_kernel(*refs):
    refs[-1][...] = jnp.concatenate([ref[...] for ref in refs[:-1]], 0)


def join(*parts):
    count = sum(part.shape[0] for part in parts)
    return local_call(join_kernel, "join", [((count, parts[0].shape[1]), BF16)], *parts)[0]


def gather_team(rows):
    before, after = ahead(rows), behind(rows)
    high, low = local_call(ends_kernel, "ends", [((64, D), BF16)] * 2, before, after)
    same = join(rows, after, before, ahead(high), behind(low))
    return same, mate(same)


def sum_team(same, other, waits=()):
    own, up, down, after_high, after_low, before_high, before_low = local_call(
        cross_kernel,
        "cross",
        [((128, D), F32)] + [((64, D), kind) for kind in (BF16, BF16, F32, BF16, BF16, F32)],
        same,
        mate(other),
        waits=waits,
        limit=60,
    )
    up, down = ahead(up), behind(down)
    after_low, before_high = ahead(after_low), behind(before_high)
    after_high, before_low = local_call(
        pass_kernel, "pass_sum", [((64, D), BF16)] * 2, after_high, up, before_low, down
    )
    return own, ahead(after_high), after_low, before_high, behind(before_low)


def sum_rows(part):
    return lax.psum_scatter(part, TEAM, scatter_dimension=0, tiled=True)


def gather_ring(rows):
    return lax.all_gather(rows, RING, axis=0, tiled=True)


def total_kernel(parts, mix_weights, ffn_grads, ffn_weights, out, sums):
    total = parts[0].astype(F32)
    for n in range(1, 16):
        total = total + parts[n].astype(F32)
    out[:1040, :] = total.astype(BF16)
    small = mix_weights[:, 768:896].astype(F32).T
    across = jnp.sum(total[768:770, :] * small[:2], 0, keepdims=True)
    rows = jnp.zeros((128, 1), F32)
    for n in range(6):
        here = slice(128 * n, 128 * n + 128)
        rows = rows + jnp.sum(total[here, :] * mix_weights[:, here].astype(F32), 1, keepdims=True)
    sums[0:1, :] = across + rows.reshape(1, 128)
    rows = jnp.zeros((128, 1), F32)
    for n in range(18):
        here = slice(128 * n, 128 * n + 128)
        grad = ffn_grads[:, here]
        out[1040 + 128 * n : 1168 + 128 * n, :] = grad
        if n % 6 < 4:
            rows = rows + jnp.sum(grad.astype(F32) * ffn_weights[:, here].astype(F32), 1, keepdims=True)
    sums[1:2, :] = rows.reshape(1, 128)


def ffn_kernel(source, *refs):
    parts, grads, stored, (active, back, second), (kept, weights, sems) = refs[:2], refs[2:4], refs[4], refs[5:8], refs[8:]
    step = pl.program_id(0)

    def copy(j):
        return pltpu.make_async_copy(stored.at[:, pl.ds(j * 768, 768)], weights.at[j], sems.at[j])

    @pl.when(step == 0)
    def _():
        for j in range(3):
            copy(j).start()

    for j in range(3):

        @pl.when(step == j)
        def _():
            copy(j).wait()
            for n, (part, grad) in enumerate(zip(parts, grads)):
                here = slice(n * 512, n * 512 + 512)
                both = dot(part[...], weights[j, :, :512], NN)
                grad_active = dot(grad[...], weights[j, :, 512:], NN)
                gate, up = both[:, :256], both[:, 256:]
                sigma = sigmoid(gate)
                swish = gate * sigma
                active[here, :] = (swish * up).astype(BF16)
                slope = sigma * (1.0 + gate * (1.0 - sigma))
                backs = jnp.concatenate([grad_active * up * slope, grad_active * swish], 1).astype(BF16)
                back[here, :] = backs
                kept[here, j * 512 : j * 512 + 512] = backs

    @pl.when(step == 2)
    def _():
        every = jnp.concatenate([weights[j, :, :512] for j in range(3)], 1)
        for n in range(2):
            done = dot(kept[n * 512 : n * 512 + 512, :], every, NT).astype(BF16)
            for q in range(4):
                second[spot(source, n * 4 + q), :] = done[q * C : q * C + C]


def ffn(source, parts, grads, weights):
    whole = [pl.BlockSpec((512, D), lambda j, source: (0, 0))] * 4
    return pl.pallas_call(
        ffn_kernel,
        grid_spec=pltpu.PrefetchScalarGridSpec(
            num_scalar_prefetch=1,
            grid=(3,),
            in_specs=whole + [pl.BlockSpec(memory_space=pl.ANY)],
            out_specs=[
                pl.BlockSpec((1024, 256), lambda j, source: (0, j)),
                pl.BlockSpec((1024, 512), lambda j, source: (0, j)),
                pl.BlockSpec((1024, D), lambda j, source: (0, 0)),
            ],
            scratch_shapes=[
                pltpu.VMEM((1024, 1536), BF16),
                pltpu.VMEM((3, D, 768), BF16),
                pltpu.SemaphoreType.DMA((3,)),
            ],
        ),
        out_shape=[
            jax.ShapeDtypeStruct((1024, 768), BF16),
            jax.ShapeDtypeStruct((1024, 1536), BF16),
            jax.ShapeDtypeStruct((1024, D), BF16),
        ],
        compiler_params=pltpu.CompilerParams(vmem_limit_bytes=60 * 1024 * 1024),
        cost_estimate=pl.CostEstimate(flops=2 * 1024 * D * 1280 * 3, bytes_accessed=30 << 20, transcendentals=0),
        name="ffn",
    )(source, *parts, *grads, weights)


def ffn_grad_kernel(*refs):
    parts, grads, (back, active, out) = refs[:2], refs[2:4], refs[4:]
    seq = jnp.concatenate([ref[...].T for ref in parts], 1)
    dy = jnp.concatenate([ref[...].T for ref in grads], 1)
    for j in range(3):
        at = j * 768
        out[:, at : at + 512] = dot(seq, back[:, j * 512 : j * 512 + 512], NN).astype(BF16)
        out[:, at + 512 : at + 768] = dot(dy, active[:, j * 256 : j * 256 + 256], NN).astype(BF16)


def ffn_grad(parts, grads, back, active):
    block = 512
    return pl.pallas_call(
        ffn_grad_kernel,
        grid=(D // block,),
        in_specs=[pl.BlockSpec((part.shape[0], block), lambda i: (0, i)) for part in (*parts, *grads)]
        + [pl.BlockSpec(part.shape, lambda i: (0, 0)) for part in (back, active)],
        out_specs=pl.BlockSpec((block, 2304), lambda i: (i, 0)),
        out_shape=jax.ShapeDtypeStruct((D, 2304), BF16),
        compiler_params=pltpu.CompilerParams(vmem_limit_bytes=60 * 1024 * 1024),
        cost_estimate=pl.CostEstimate(flops=2 * 1024 * D * 2304, bytes_accessed=20 << 20, transcendentals=0),
        name="ffn_grad",
    )(*parts, *grads, back, active)


def in_grad_kernel(one, back, taps, near, other, mixed, out):
    total = dot(one[...], back[...], NN)
    outer = 0.0
    at = 0
    for ref in (near, other):
        outer = outer + dot(mixed[at : at + ref.shape[0], :].T, ref[...], NN)
        at += ref.shape[0]
    small = total[:, 768:].T
    every = jnp.concatenate([taps[...], jnp.zeros((96, C), F32)], 0).astype(BF16)
    lane = lax.broadcasted_iota(jnp.int32, (8, C), 1)
    for r in range(4):
        rows = slice(r * 128, r * 128 + 128)
        for n in range(6):
            out[r, n * 128 : n * 128 + 128, :] = total[rows, n * 128 : n * 128 + 128].astype(BF16)
        chosen = lane == place_of(pl.program_id(0) * 4 + r) * 8 + lax.broadcasted_iota(jnp.int32, (8, C), 0)
        picked = dot(jnp.where(chosen, 1.0, 0.0).astype(BF16), every, NT)
        tail = jnp.concatenate([small[:2, rows], picked, jnp.zeros((6, 128), F32)], 0)
        out[r, 768:784, :] = tail.astype(BF16)
        out[r, 784:, :] = outer[:, rows].astype(BF16)


def in_grad(one, back, taps, three, mixed):
    block = 512
    return pl.pallas_call(
        in_grad_kernel,
        grid=(D // block,),
        in_specs=[
            pl.BlockSpec((block, 1024), lambda i: (i, 0)),
            pl.BlockSpec(back.shape, lambda i: (0, 0)),
            pl.BlockSpec((32, C), lambda i: (0, 0)),
            *[pl.BlockSpec((part.shape[0], block), lambda i: (0, i)) for part in three],
            pl.BlockSpec(mixed.shape, lambda i: (0, 0)),
        ],
        out_specs=pl.BlockSpec((4, 1040, 128), lambda i: (i, 0, 0)),
        out_shape=jax.ShapeDtypeStruct((16, 1040, 128), BF16),
        compiler_params=pltpu.CompilerParams(vmem_limit_bytes=60 * 1024 * 1024),
        cost_estimate=pl.CostEstimate(flops=2 * 1024 * D * 1152, bytes_accessed=8 << 20, transcendentals=0),
        name="in_grad",
    )(one, back, taps, *three, mixed)


def first_kernel_parts(back, weights, *outs):
    at = 0
    for out in outs:
        count = out.shape[0]
        out[...] = dot(back[at : at + count, :], weights[...], NT).astype(BF16)
        at += count


def first_parts(back, weights):
    block = 512
    return pl.pallas_call(
        first_kernel_parts,
        grid=(D // block,),
        in_specs=[pl.BlockSpec((1024, 896), lambda i: (0, 0)), pl.BlockSpec((block, 896), lambda i: (i, 0))],
        out_specs=[pl.BlockSpec((count, block), lambda i: (0, i)) for count in PARTS],
        out_shape=[jax.ShapeDtypeStruct((count, D), BF16) for count in PARTS],
        compiler_params=pltpu.CompilerParams(vmem_limit_bytes=60 * 1024 * 1024),
        cost_estimate=pl.CostEstimate(flops=2 * 1024 * D * 896, bytes_accessed=8 << 20, transcendentals=0),
        name="first_parts",
    )(back, weights)


def down_kernel(active, first, second, third, wait, *outs):
    right = jnp.concatenate([first[...], second[...], third[...]], 1)
    at = 0
    for out in outs:
        out[...] = dot(active[at : at + out.shape[0], :], right, NT).astype(BF16)
        at += out.shape[0]


def down_product(active, weights, wait):
    block = 512
    return pl.pallas_call(
        down_kernel,
        grid=(D // block,),
        in_specs=[pl.BlockSpec((1024, PAD), lambda i: (0, 0))]
        + [pl.BlockSpec((block, 256), lambda i, j=j: (i, 3 * j + 2)) for j in range(3)]
        + [pl.BlockSpec(memory_space=pl.ANY)],
        out_specs=[pl.BlockSpec((count, block), lambda i: (0, i)) for count in PARTS],
        out_shape=[jax.ShapeDtypeStruct((count, D), BF16) for count in PARTS],
        compiler_params=pltpu.CompilerParams(vmem_limit_bytes=60 * 1024 * 1024),
        cost_estimate=pl.CostEstimate(flops=2 * 1024 * D * 768, bytes_accessed=8 << 20, transcendentals=0),
        name="down_product",
    )(active, weights, weights, weights, wait)


def team_total(values):
    values = values.reshape(2, 4, 2, 16)
    core = lax.axis_index("c")
    mine = lax.dynamic_index_in_dim(values, core, 2, False)
    mine = mine + mate(lax.dynamic_index_in_dim(values, 1 - core, 2, False))
    place = lax.axis_index("z")
    total = 0.0
    for distance in range(4):
        block = lax.dynamic_index_in_dim(mine, (place + distance) & 3, 1, False)
        pairs = [
            ((c * 4 + n) * 2 + y, (y * 4 + (n + distance) % 4) * 2 + c)
            for c in range(2)
            for n in range(4)
            for y in range(2)
        ]
        total = total + lax.ppermute(block, ("c", "z", "yl"), pairs)
    return total


def on_device(
    tokens,
    segments,
    cotangent,
    attn_gain,
    w_query,
    w_key,
    w_value,
    w_beta,
    conv_weight,
    w_out,
    ffn_gain,
    w_gate,
    w_up,
    w_down,
):
    core, z = lax.axis_index("c"), lax.axis_index("z")
    true = jnp.arange(8, dtype=jnp.int32)
    distance, other = (true // 2 - z) & 3, (true % 2) ^ core
    place = (jnp.where(distance > 1, 5 - distance, distance) + 4 * other).astype(jnp.int32)

    source = jnp.sum(jnp.where(place[:, None] == true[None, :], true[:, None], 0), 0).astype(jnp.int32)

    mix_pack, gains = local_call(
        mix_pack_kernel,
        "mix_pack",
        [((128, 1152 + D), BF16), ((16, 2, 16), F32)],
        w_query,
        w_key,
        w_value,
        w_beta.T,
        conv_weight.reshape(24, 8),
        segments.reshape(8, 128),
        w_out,
        attn_gain.reshape(1, 16),
        ffn_gain.reshape(1, 16),
        tokens,
        limit=60,
    )
    mix_pack = trade(mix_pack)
    rows, one = local_call(norm_kernel, "norm_one", [((128, D), BF16)] * 2, mix_pack)
    (grad_rows,) = local_call(order_kernel, "order_grad", [((128, D), BF16)], cotangent, limit=60)
    grad_rows = trade(grad_rows)
    (ffn_pack,) = local_call(ffn_pack_kernel, "ffn_pack", [((128, 2304), BF16)], w_gate.T, w_up.T, w_down, limit=60)
    ffn_pack = trade(ffn_pack)

    gains = lax.all_to_all(gains, ("z", "yl", "c"), 0, 0, tiled=True).reshape(8, 2, 2, 16)
    gains = gains.transpose(1, 2, 0, 3).reshape(2, 2, 128)
    home = jnp.where(core == 0, gains[0], gains[1])
    away = jnp.where(lax.axis_index("yl") == 0, gains[0], gains[1])
    (scaled_pack,) = local_call(mix_scale_kernel, "mix_scale", [((128, 1152), BF16)], mix_pack, away[0][:, None])
    mix_w = gather_ring(scaled_pack)

    one = gather_team(one)
    grads = gather_team(grad_rows)
    (scaled_ffn,) = local_call(
        ffn_scale_kernel, "ffn_scale", [((128, 2304), BF16)], ffn_pack, away[1][:, None]
    )
    ffn_w = gather_ring(scaled_ffn)

    marks, seg_rows = local_call(marks_kernel, "marks", [((1024, 128), F32), ((8, 128), F32)], mix_pack)
    mixed, raw, taps, *saved = mix_forward(place, one, mix_w, marks, seg_rows, (scaled_ffn, grads[1]))
    middle, two = local_call(
        middle_kernel, "middle", [((128, D), F32), ((128, D), BF16)], rows, *sum_team(*saved[:2])
    )
    one_turned = turned(one, saved[0])
    two = gather_team(two)
    active, ffn_back, second = ffn(source, two, grads, ffn_w)
    ffn_grads = ffn_grad(two, grads, ffn_back, active)
    result = down_product(active, ffn_w, second)
    middle_grad, three = local_call(
        second_kernel,
        "second",
        [((128, D), F32), ((128, D), BF16)],
        middle,
        grad_rows,
        sum_rows(second),
        waits=(ffn_grads, one_turned, result[0]),
    )
    ring_grads = lax.psum_scatter(ffn_grads, RING, scatter_dimension=0, tiled=True)
    three = gather_team(three)
    back, taps_grad = mix_backward(place, three, mix_w, raw, taps, marks, seg_rows, saved[2:])
    ring_parts = lax.all_to_all(in_grad(one_turned, back, taps_grad, three, mixed), RING, 0, 0, tiled=True)
    terms = sum_team(*first_parts(back, mix_w))
    (tokens_grad,) = local_call(first_kernel, "first", [((128, D), BF16)], rows, middle_grad, *terms)
    (tokens_grad,) = local_call(widen_kernel, "widen", [((128, D), F32)], trade(tokens_grad))
    terms = sum_team(*result, waits=terms[:1])
    (output,) = local_call(result_kernel, "result", [((128, D), BF16)], middle, *terms)
    output = trade(output)
    total, sums = local_call(
        total_kernel,
        "ring_total",
        [((1040 + 2304, 128), BF16), ((2, 128), F32)],
        ring_parts,
        scaled_pack,
        ring_grads,
        scaled_ffn,
        waits=(tokens_grad, output),
    )
    total, sums = trade(total), team_total(sums)
    grad_gate, grad_up, grad_down = local_call(
        ffn_unpack_kernel, "ffn_unpack", [((HID, 128), F32)] * 3, total, home[1][None]
    )
    grad_query, grad_key, grad_value, grad_beta, grad_taps, grad_out = local_call(
        mix_unpack_kernel,
        "mix_unpack",
        [((128, 256), F32)] * 3 + [((2, 128), F32), ((8, 128), F32), ((256, 128), F32)],
        total,
        home[0][:, None],
    )
    grad_taps = grad_taps[:, :24].reshape(8, 3, 4, 2).transpose(1, 2, 3, 0)
    return (
        output,
        tokens_grad,
        sums[0] / attn_gain,
        grad_query,
        grad_key,
        grad_value,
        grad_beta.T,
        grad_taps,
        grad_out,
        sums[1] / ffn_gain,
        grad_gate.T,
        grad_up.T,
        grad_down,
    )


def solution(mesh):
    dp, tensor = ("yh", "x", "c"), ("z", "yl")
    every = dp + tensor
    split = jax.sharding.Mesh(mesh.devices.reshape(2, 4, 2, 4, 2), AXES)
    placed = (
        P(every, None),
        P(dp),
        P(every, None),
        P(every),
        P(dp, tensor),
        P(dp, tensor),
        P(dp, tensor),
        P(dp, tensor),
        P(None, None, tensor, dp),
        P(tensor, dp),
        P(every),
        P(dp, tensor),
        P(dp, tensor),
        P(tensor, dp),
    )
    return jax.shard_map(
        on_device,
        mesh=split,
        in_specs=placed,
        out_specs=(
            P(every, None),
            P(every, None),
            P(every),
            P(dp, tensor),
            P(dp, tensor),
            P(dp, tensor),
            P(dp, tensor),
            P(None, None, tensor, dp),
            P(tensor, dp),
            P(every),
            P(dp, tensor),
            P(dp, tensor),
            P(tensor, dp),
        ),
        check_vma=False,
    )
```

```python
import functools
import jax
import jax.numpy as jnp
from jax import lax
from jax.experimental import pallas as pl
from jax.experimental.pallas import tpu as pltpu
from jax.sharding import PartitionSpec as P

C = 128
D = 2048
PARTS = (512, 512)
EPS = 1e-06
F32 = jnp.float32
BF16 = jnp.bfloat16
NN = (((1,), (0,)), ((), ()))
NT = (((1,), (1,)), ((), ()))
TN = (((0,), (0,)), ((), ()))


def dot(left, right, dims):
    return lax.dot_general(left, right, dims, preferred_element_type=F32)


def halves(value):
    high = value.astype(BF16)
    return high, (value - high.astype(F32)).astype(BF16)


def fine(left, right, dims):
    left_high, left_low = halves(left)
    right_high, right_low = halves(right)
    (over,), (under,) = dims[0]
    first = dot(
        jnp.concatenate([left_high, left_low], over), jnp.concatenate([right_high, right_high], under), dims
    )
    return first + dot(left_high, right_low, dims)


def sigmoid(v):
    return 1.0 / (1.0 + jnp.exp(-v))


def masks():
    row = lax.broadcasted_iota(jnp.int32, (C, C), 0)
    col = lax.broadcasted_iota(jnp.int32, (C, C), 1)
    return row, col


def shifted(rows, before, offset):
    joined = jnp.concatenate([before, rows], 0)
    return pltpu.roll(joined, offset, 0)[8:]


def convolved(rows, before, taps, marks):
    total = taps[0] * rows
    moved = []
    for offset in range(1, 4):
        term = shifted(rows, before, offset) * marks[offset - 1]
        moved.append(term)
        total = total + taps[offset] * term
    return total, moved


def inverses(systems):
    row, col = masks()
    eye = jnp.where(row == col, 1.0, 0.0)
    solved = []
    near = (row == col + 1) & ((row & 1) == 1)
    solved = [eye - jnp.where(near, a, 0.0) for a in systems]
    for level in range(1, 7):
        odd = ((row >> level) & 1) == 1
        off = odd & ((row >> level) == (col >> level) + 1)
        parts = [fine(x, jnp.where(off, a, 0.0), NN) for x, a in zip(solved, systems)]
        solved = [x - fine(p, x, NN) for x, p in zip(solved, parts)]
    return solved


def taps_of(taps, part, h):
    return [taps[row : row + 1] for row in range(part * 8 + h, part * 8 + 8, 2)]


def place_of(member):
    return (member // 8 * 4 + member % 4) * 2 + member // 4 % 2


def gathered_taps(weights):
    lane = lax.broadcasted_iota(jnp.int32, (C, C), 0)
    target = lax.broadcasted_iota(jnp.int32, (C, C), 1)
    total = jnp.zeros((32, C), F32)
    for member in range(16):
        chosen = (lane >= 8) & (lane < 16) & (target == lane - 8 + place_of(member) * 8)
        piece = weights[member * C : member * C + 32, 768:]
        total = total + dot(piece, jnp.where(chosen, 1.0, 0.0).astype(BF16), NN)
    return total


def forward_kernel(chunks, mm, place, same, other, weights, out_w, out_w_next, aux, segs, wait, wait_next, mixed, raw, taps, part_same, part_other, t_out, u_out, s_out, m_out, q_out, before, state):
    step = pl.program_id(0)

    @pl.when(step == 0)
    def _():
        raw[:512, :] = dot(same[...], weights[...], NN)
        raw[512:, :] = dot(other[...], weights[...], NN)
        taps[...] = gathered_taps(weights)
        before[...] = jnp.zeros_like(before)
        state[...] = jnp.zeros_like(state)

    row, col = masks()
    eye = jnp.where(row == col, 1.0, 0.0)
    taps_now = taps[...]
    items = []
    for c in range(chunks):
        rows, fixed = spot(place, chunks * step + c), pl.ds(c * C, C)
        prev = before[...] if c == 0 else raw[spot(place, chunks * step + c - 1, 120, 8), :768]
        marks = [aux[fixed, j : j + 1] for j in range(3)]
        carried, closing, seg = aux[fixed, 3:4], aux[fixed, 4:5], aux[fixed, 5:6]
        same_doc = seg == segs[0, c : c + 1, :]
        gamma = carried[C - 1 : C]
        for h in range(2):
            acts = []
            for part in range(3):
                cols = slice(384 * h + 128 * part, 384 * h + 128 * part + 128)
                conv, _ = convolved(raw[rows, cols], prev[:, cols], taps_of(taps_now, part, h), marks)
                acts.append(conv * sigmoid(conv))
            q, k, v = acts
            q = q * lax.rsqrt(jnp.sum(q * q, -1, keepdims=True) + EPS)
            k = k * lax.rsqrt(jnp.sum(k * k, -1, keepdims=True) + EPS)
            b = sigmoid(raw[rows, 768 + h : 769 + h])
            items.append((q, k, v, b, carried, closing, same_doc, gamma))
    before[...] = raw[spot(place, chunks * step + chunks - 1, 120, 8), :768]
    systems, scores = [], []
    for q, k, v, b, carried, closing, same_doc, gamma in items:
        gram = mm(k, k, NT)
        systems.append(jnp.where(same_doc & (row > col), b * gram, 0.0))
        scores.append(jnp.where(same_doc & (row >= col), mm(q, k, NT), 0.0))
    solved = inverses(systems)
    wus = [
        mm(t, jnp.concatenate([(i[4] * i[3]) * i[1], i[3] * i[2]], 1), NN)
        for t, i in zip(solved, items)
    ]
    mns = [mm(i[5] * i[1], wu, TN) for wu, i in zip(wus, items)]
    qos = [mm(p, wu, NN) for p, wu in zip(scores, wus)]
    for n, i in enumerate(items):
        c, h = n // 2, n % 2
        t_out[h, c] = solved[n]
        now = state[h]
        s_out[h, c] = now
        move = i[7] * eye - mns[n][:, :128]
        query = i[4] * i[0] - qos[n][:, :128]
        m_out[h, c] = move
        q_out[h, c] = query
        state[h] = mm(move, now, NN) + mns[n][:, 128:]
        u_out[h, c] = wus[n][:, 128:] - mm(wus[n][:, :128], now, NN)
        result = (mm(query, now, NN) + qos[n][:, 128:]).astype(BF16)
        mixed[spot(place, chunks * step + c), h * 128 : h * 128 + 128] = result

    @pl.when(step == pl.num_programs(0) - 1)
    def _():
        project = jnp.concatenate([out_w[...], out_w_next[...]], 1)
        at = 0
        for ref in (part_same, part_other):
            count = ref.shape[0]
            ref[...] = dot(mixed[at : at + count, :], project, NT).astype(BF16)
            at += count


def spot(place, block, start=0, count=C):
    return pl.ds(pl.multiple_of(place[block] * C + start, 8), count)


def mix_forward(place, parts, weights, aux, segs, waits, mm=fine):
    chunks, steps = 8, 1
    saved = jax.ShapeDtypeStruct((2, 8, C, C), F32)
    block = pl.BlockSpec((2, chunks, C, C), lambda i, place: (0, i, 0, 0))
    rows = lambda width: pl.BlockSpec((1024, width), lambda i, place: (0, 0))
    return pl.pallas_call(
        functools.partial(forward_kernel, chunks, mm),
        grid_spec=pltpu.PrefetchScalarGridSpec(
            num_scalar_prefetch=1,
            grid=(steps,),
            in_specs=[
                *[pl.BlockSpec((part.shape[0], D), lambda i, place: (0, 0)) for part in parts],
                pl.BlockSpec((D, 896), lambda i, place: (0, 0)),
                *[pl.BlockSpec((D, 128), lambda i, place, n=n: (0, 7 + n)) for n in range(2)],
                pl.BlockSpec((chunks * C, 128), lambda i, place: (i, 0)),
                pl.BlockSpec((1, chunks, 128), lambda i, place: (i, 0, 0)),
                *[pl.BlockSpec(memory_space=pl.ANY) for _ in waits],
            ],
            out_specs=[rows(256), rows(896), pl.BlockSpec((32, C), lambda i, place: (0, 0))]
            + [pl.BlockSpec((count, D), lambda i, place: (0, 0)) for count in PARTS]
            + [block] * 5,
            scratch_shapes=[pltpu.VMEM((8, 768), F32), pltpu.VMEM((2, C, C), F32)],
        ),
        out_shape=[jax.ShapeDtypeStruct((1024, 256), BF16)]
        + [jax.ShapeDtypeStruct((1024, 896), F32), jax.ShapeDtypeStruct((32, C), F32)]
        + [jax.ShapeDtypeStruct((count, D), BF16) for count in PARTS]
        + [saved] * 5,
        compiler_params=pltpu.CompilerParams(vmem_limit_bytes=60 * 1024 * 1024),
        cost_estimate=pl.CostEstimate(flops=20 << 30, bytes_accessed=20 << 20, transcendentals=0),
        name="mix_forward",
    )(place, *parts, weights, weights, weights, aux, segs.reshape(steps, chunks, 128), *waits)


def backward_kernel(chunks, mm, place, near, other, out_w, out_w_next, raw, taps, aux, segs, t_in, u_in, s_in, m_in, q_in, back, taps_grad, after, adjoint, grad):
    step = pl.program_id(0)
    last = pl.num_programs(0) - 1
    start = chunks * (last - step)

    @pl.when(step == 0)
    def _():
        weights = jnp.concatenate([out_w[...], out_w_next[...]], 1)
        at = 0
        for ref in (near, other):
            grad[at : at + ref.shape[0], :] = dot(ref[...], weights, NN)
            at += ref.shape[0]
        after[...] = jnp.zeros_like(after)
        adjoint[...] = jnp.zeros_like(adjoint)
        taps_grad[...] = jnp.zeros_like(taps_grad)
        back[:, 768:] = jnp.zeros_like(back[:, 768:])

    row, col = masks()
    taps_now = taps[...]
    taps_sum = [[jnp.zeros((1, 128), F32) for _ in range(4)] for _ in range(6)]
    items = []
    for c in range(chunks):
        rows, fixed = spot(place, start + c), pl.ds(c * C, C)
        if c == 0:
            prev = jnp.where(step == last, 0.0, raw[spot(place, jnp.maximum(start - 1, 0), 120, 8), :768])
        else:
            prev = raw[spot(place, start + c - 1, 120, 8), :768]
        marks = [aux[fixed, j : j + 1] for j in range(3)]
        carried, closing, seg = aux[fixed, 3:4], aux[fixed, 4:5], aux[fixed, 5:6]
        same = seg == segs[0, c : c + 1, :]
        for h in range(2):
            acts, slopes, moved = [], [], []
            for part in range(3):
                cols = slice(384 * h + 128 * part, 384 * h + 128 * part + 128)
                now = raw[rows, cols]
                conv, terms = convolved(now, prev[:, cols], taps_of(taps_now, part, h), marks)
                s = sigmoid(conv)
                acts.append(conv * s)
                slopes.append(s * (1.0 + conv * (1.0 - s)))
                moved.append([now] + terms)
            q, k, v = acts
            rq = lax.rsqrt(jnp.sum(q * q, -1, keepdims=True) + EPS)
            rk = lax.rsqrt(jnp.sum(k * k, -1, keepdims=True) + EPS)
            b = sigmoid(raw[rows, 768 + h : 769 + h])
            do = grad[rows, 128 * h : 128 * h + 128]
            items.append((c, h, marks, carried, closing, same, slopes, moved, q * rq, k * rk, v, b, rq, rk, do))
    for item in sorted(items, key=lambda item: (-item[0], item[1])):
        c, h, marks, carried, closing, same, slopes, moved, q, k, v, b, rq, rk, do = item
        t, u, s, m, qe = t_in[h, c], u_in[h, c], s_in[h, c], m_in[h, c], q_in[h, c]
        g = adjoint[h]
        adjoint[h] = mm(m, g, TN) + mm(qe, do, TN)
        gram = mm(k, k, NT)
        score = jnp.where(same & (row >= col), mm(q, k, NT), 0.0)
        du = mm(score, do, TN) + mm(closing * k, g, NN)
        dr = mm(t, du, TN)
        dps = mm(jnp.concatenate([do, dr], 0), u, NT)
        dp = jnp.where(same & (row >= col), dps[:C], 0.0)
        da = jnp.where(same & (row > col), -dps[C:], 0.0)
        e = b * da
        sides = mm(jnp.concatenate([carried * do, (carried * b) * dr], 0), s, NT)
        inner = mm(jnp.concatenate([dp, e], 0), k, NN)
        dq = sides[:C] + inner[:C]
        dk = (
            inner[C:]
            - sides[C:]
            + mm(jnp.concatenate([dp, e], 0), jnp.concatenate([q, k], 0), TN)
            + closing * mm(u, g, NT)
        )
        ks = mm(k, s, NN)
        db = jnp.sum(dr * (v - carried * ks) + da * gram, -1, keepdims=True)
        backs = (
            rq * (dq - q * jnp.sum(dq * q, -1, keepdims=True)),
            rk * (dk - k * jnp.sum(dk * k, -1, keepdims=True)),
            b * dr,
        )
        rows = spot(place, start + c)
        back[rows, 768 + h : 769 + h] = (db * b * (1.0 - b)).astype(BF16)
        for part in range(3):
            d = backs[part] * slopes[part]
            cols = slice(384 * h + part * 128, 384 * h + part * 128 + 128)
            sums = taps_sum[3 * h + part]
            taps_here = taps_of(taps_now, part, h)
            total = taps_here[0] * d
            sums[0] += jnp.sum(d * moved[part][0], 0, keepdims=True)
            for offset in range(1, 4):
                sums[offset] += jnp.sum(d * moved[part][offset], 0, keepdims=True)
                marked = d * marks[offset - 1]
                joined = jnp.concatenate([marked, after[offset - 1, :, cols]], 0)
                after[offset - 1, :, cols] = marked[:8]
                up = pltpu.roll(joined, C + 8 - offset, 0)[:C]
                total = total + taps_here[offset] * up
            back[rows, cols] = total.astype(BF16)
    for n in range(6):
        for offset in range(4):
            at = (n % 3 * 4 + offset) * 2 + n // 3
            taps_grad[at : at + 1, :] += taps_sum[n][offset]


def mix_backward(place, three, weights, raw, taps, aux, segs, saved, mm=fine):
    chunks, steps = 2, 4
    block = pl.BlockSpec((2, chunks, C, C), lambda i, place: (0, steps - 1 - i, 0, 0))
    rows = lambda width: pl.BlockSpec((1024, width), lambda i, place: (0, 0))
    return pl.pallas_call(
        functools.partial(backward_kernel, chunks, mm),
        grid_spec=pltpu.PrefetchScalarGridSpec(
            num_scalar_prefetch=1,
            grid=(steps,),
            in_specs=[pl.BlockSpec(part.shape, lambda i, place: (0, 0)) for part in three]
            + [pl.BlockSpec((D, 128), lambda i, place, n=n: (0, 7 + n)) for n in range(2)]
            + [
                rows(896),
                pl.BlockSpec((32, C), lambda i, place: (0, 0)),
                pl.BlockSpec((chunks * C, 128), lambda i, place: (steps - 1 - i, 0)),
                pl.BlockSpec((1, chunks, 128), lambda i, place: (steps - 1 - i, 0, 0)),
            ]
            + [block] * 5,
            out_specs=[rows(896), pl.BlockSpec((32, C), lambda i, place: (0, 0))],
            scratch_shapes=[
                pltpu.VMEM((3, 8, 768), F32),
                pltpu.VMEM((2, C, C), F32),
                pltpu.VMEM((1024, 256), F32),
            ],
        ),
        out_shape=[jax.ShapeDtypeStruct((1024, 896), BF16), jax.ShapeDtypeStruct((32, C), F32)],
        compiler_params=pltpu.CompilerParams(vmem_limit_bytes=60 * 1024 * 1024),
        cost_estimate=pl.CostEstimate(flops=25 << 30, bytes_accessed=20 << 20, transcendentals=0),
        name="mix_backward",
    )(place, *three, weights, weights, raw, taps, aux, segs.reshape(steps, chunks, 128), *saved)


def marks_kernel(pack, aux, rows):
    segs = pack[:, 784:792].astype(F32)
    rows[...] = segs.T
    aux[...] = jnp.zeros_like(aux)
    for c in range(8):
        now = jnp.broadcast_to(segs[:, c : c + 1], (C, C))
        prior = jnp.broadcast_to(segs[:, c - 1 : c], (C, C)) if c else jnp.full((C, C), -1.0, F32)
        joined = jnp.concatenate([prior[120:], now], 0)
        columns = [pltpu.roll(joined, offset, 0)[8:] == now for offset in range(1, 4)]
        columns += [now == prior[C - 1 : C], now == now[C - 1 : C]]
        here = pl.ds(c * C, C)
        for n, column in enumerate(columns):
            aux[here, n : n + 1] = jnp.where(column, 1.0, 0.0)[:, :1]
        aux[here, 5:6] = now[:, :1]


AXES = ("yh", "x", "c", "z", "yl")
TEAM = ("z", "c")
RING = ("yh", "yl", "x")
PAD = 768
HID = 704
FORTH = [(a * 4 + x) * 2 + p for a in range(2) for p in range(2) for x in range(4)]
HOME = [(a * 2 + p) * 4 + x for a in range(2) for x in range(4) for p in range(2)]


def trade(value):
    return lax.ppermute(value, ("c", "yl"), [(0, 0), (1, 2), (2, 1), (3, 3)])


def mate(value):
    return lax.ppermute(value, "c", [(0, 1), (1, 0)])


def ahead(value):
    return lax.ppermute(value, "z", [(n, (n + 1) % 4) for n in range(4)])


def behind(value):
    return lax.ppermute(value, "z", [(n, (n - 1) % 4) for n in range(4)])


def local_call(kernel, name, outs, *operands, waits=(), limit=48):
    count = len(operands)

    def body(*refs):
        kernel(*refs[:count], *refs[count + len(waits) :])

    def whole(shape):
        return pl.BlockSpec(shape, lambda i: (0,) * len(shape))

    return pl.pallas_call(
        body,
        grid=(1,),
        in_specs=[whole(part.shape) for part in operands] + [pl.BlockSpec(memory_space=pl.ANY)] * len(waits),
        out_specs=[whole(shape) for shape, _ in outs],
        out_shape=[jax.ShapeDtypeStruct(shape, kind) for shape, kind in outs],
        compiler_params=pltpu.CompilerParams(vmem_limit_bytes=limit * 1024 * 1024),
        name=name,
    )(*operands, *waits)


def inverse_rms(rows):
    return lax.rsqrt(jnp.mean(rows * rows, -1, keepdims=True) + EPS)


def norm_back(normed, scale, scaled):
    return scale * (scaled - normed * jnp.mean(scaled * normed, -1, keepdims=True))


def put(out, value, blocks, at=0):
    for n, block in enumerate(blocks):
        out[:, at + n * 128 : at + n * 128 + 128] = value[:, block * 128 : block * 128 + 128].astype(out.dtype)


def norm_kernel(pack, rows, out):
    value = pack[:, 1152:].astype(F32)
    put(rows, value, FORTH)
    put(out, value * inverse_rms(value), FORTH)


def order_kernel(rows, out):
    put(out, rows[...], FORTH)


def ends_kernel(before, after, high, low):
    high[...] = before[:64]
    low[...] = after[64:]


def turn_kernel(*refs):
    at = 0
    for ref in refs[:2]:
        refs[-1][:, at : at + ref.shape[0]] = ref[...].T
        at += ref.shape[0]


def turned(parts, wait):
    block = 512
    return pl.pallas_call(
        turn_kernel,
        grid=(D // block,),
        in_specs=[pl.BlockSpec((part.shape[0], block), lambda i: (0, i)) for part in parts]
        + [pl.BlockSpec(memory_space=pl.ANY)],
        out_specs=pl.BlockSpec((block, 1024), lambda i: (i, 0)),
        out_shape=jax.ShapeDtypeStruct((D, 1024), BF16),
        compiler_params=pltpu.CompilerParams(vmem_limit_bytes=60 * 1024 * 1024),
        name="turned",
    )(*parts, wait)


def landed(own, up_high, up_low, down_high, down_low):
    high = up_high[...].astype(F32) + down_high[...].astype(F32)
    low = up_low[...].astype(F32) + down_low[...].astype(F32)
    return own[...] + jnp.concatenate([high, low], 0)


def middle_kernel(rows, own, up_high, up_low, down_high, down_low, middle, normed):
    value = rows[...].astype(F32) + landed(own, up_high, up_low, down_high, down_low)
    middle[...] = value
    normed[...] = (value * inverse_rms(value)).astype(BF16)


def second_kernel(middle, grad, scaled, out, low):
    value = middle[...]
    scale = inverse_rms(value)
    total = grad[...].astype(F32) + norm_back(value * scale, scale, scaled[...].astype(F32))
    out[...] = total
    low[...] = total.astype(BF16)


def first_kernel(rows, grad, own, up_high, up_low, down_high, down_low, out):
    value = rows[...].astype(F32)
    scale = inverse_rms(value)
    scaled = landed(own, up_high, up_low, down_high, down_low)
    put(out, grad[...] + norm_back(value * scale, scale, scaled), HOME)


def widen_kernel(rows, out):
    out[...] = rows[...].astype(F32)


def result_kernel(middle, own, up_high, up_low, down_high, down_low, out):
    put(out, middle[...] + landed(own, up_high, up_low, down_high, down_low), HOME)


def mix_pack_kernel(query, key, value, beta, taps, segs, out_w, gain_one, gain_two, tokens, out, gains):
    for n, ref in enumerate((query, key, value)):
        for h in range(2):
            out[:, h * 384 + n * 128 : h * 384 + n * 128 + 128] = ref[:, h * 128 : h * 128 + 128]
    out[:, 768:896] = jnp.zeros((128, 128), BF16)
    out[:, 768:776] = jnp.concatenate([beta[...].astype(F32), jnp.zeros((6, 128), F32)], 0).T.astype(BF16)
    out[:24, 776:784] = taps[...]
    out[:, 784:792] = segs[...].astype(F32).T.astype(BF16)
    out[:, 896:1152] = out_w[...].astype(F32).T.astype(BF16)
    for n in range(16):
        gains[n] = jnp.concatenate([gain_one[...], gain_two[...]], 0)
    out[:, 1152:] = tokens[...]


def mix_scale_kernel(pack, gain, out):
    out[:, :768] = (pack[:, :768].astype(F32) * gain[...]).astype(BF16)
    small = pack[:, 768:896].astype(F32)
    lane = lax.broadcasted_iota(jnp.int32, small.shape, 1)
    out[:, 768:896] = jnp.where(lane < 2, small * gain[...], small).astype(BF16)
    out[:, 896:] = pack[:, 896:1152]


def ffn_pack_kernel(gate, up, down, out):
    for n, ref in enumerate((gate, up, down)):
        for j in range(3):
            count = min(256, HID - 256 * j)
            at = 768 * j + 256 * n
            out[:, at : at + count] = ref[256 * j : 256 * j + count, :].astype(F32).T.astype(BF16)
            if count < 256:
                out[:, at + count : at + 256] = jnp.zeros((128, 256 - count), BF16)


def ffn_scale_kernel(pack, gain, out):
    for j in range(3):
        at = 768 * j
        out[:, at : at + 512] = (pack[:, at : at + 512].astype(F32) * gain[...]).astype(BF16)
        out[:, at + 512 : at + 768] = pack[:, at + 512 : at + 768]


def ffn_unpack_kernel(pack, gain, gate, up, down):
    for n, ref in enumerate((gate, up, down)):
        for block in range(6):
            count = min(128, HID - 128 * block)
            at = 1040 + 768 * (block // 2) + 256 * n + 128 * (block % 2)
            value = pack[at : at + 128, :].astype(F32).T[:count]
            ref[128 * block : 128 * block + count, :] = value if n == 2 else value * gain[...]


def mix_unpack_kernel(pack, gain, query, key, value, beta, taps, out):
    for h in range(2):
        for n, ref in enumerate((query, key, value)):
            at = 384 * h + 128 * n
            ref[:, h * 128 : h * 128 + 128] = pack[at : at + 128, :].astype(F32) * gain[...]
    beta[...] = pack[768:784, :].astype(F32)[:2] * gain[...].reshape(1, 128)
    taps[...] = pack[768:784, :].astype(F32)[2:10]
    out[...] = pack[784:1040, :].astype(F32)


def cross_kernel(same, other, own, up, down, after_high, after_low, before_high, before_low):
    total = same[...].astype(F32) + other[...].astype(F32)
    own[...] = total[:128]
    after_high[...] = total[128:192]
    after_low[...] = total[192:256].astype(BF16)
    before_high[...] = total[256:320].astype(BF16)
    before_low[...] = total[320:384]
    up[...] = total[384:448].astype(BF16)
    down[...] = total[448:].astype(BF16)


def pass_kernel(high, up, low, down, after, before):
    after[...] = (high[...] + up[...].astype(F32)).astype(BF16)
    before[...] = (low[...] + down[...].astype(F32)).astype(BF16)


def join_kernel(*refs):
    refs[-1][...] = jnp.concatenate([ref[...] for ref in refs[:-1]], 0)


def join(*parts):
    count = sum(part.shape[0] for part in parts)
    return local_call(join_kernel, "join", [((count, parts[0].shape[1]), BF16)], *parts)[0]


def gather_team(rows):
    before, after = ahead(rows), behind(rows)
    high, low = local_call(ends_kernel, "ends", [((64, D), BF16)] * 2, before, after)
    same = join(rows, after, before, ahead(high), behind(low))
    return same, mate(same)


def sum_team(same, other, waits=()):
    own, up, down, after_high, after_low, before_high, before_low = local_call(
        cross_kernel,
        "cross",
        [((128, D), F32)] + [((64, D), kind) for kind in (BF16, BF16, F32, BF16, BF16, F32)],
        same,
        mate(other),
        waits=waits,
        limit=60,
    )
    up, down = ahead(up), behind(down)
    after_low, before_high = ahead(after_low), behind(before_high)
    after_high, before_low = local_call(
        pass_kernel, "pass_sum", [((64, D), BF16)] * 2, after_high, up, before_low, down
    )
    return own, ahead(after_high), after_low, before_high, behind(before_low)


def sum_rows(part):
    return lax.psum_scatter(part, TEAM, scatter_dimension=0, tiled=True)


def gather_ring(rows):
    return lax.all_gather(rows, RING, axis=0, tiled=True)


def total_kernel(parts, mix_weights, ffn_grads, ffn_weights, out, sums):
    total = parts[0].astype(F32)
    for n in range(1, 16):
        total = total + parts[n].astype(F32)
    out[:1040, :] = total.astype(BF16)
    small = mix_weights[:, 768:896].astype(F32).T
    across = jnp.sum(total[768:770, :] * small[:2], 0, keepdims=True)
    rows = jnp.zeros((128, 1), F32)
    for n in range(6):
        here = slice(128 * n, 128 * n + 128)
        rows = rows + jnp.sum(total[here, :] * mix_weights[:, here].astype(F32), 1, keepdims=True)
    sums[0:1, :] = across + rows.reshape(1, 128)
    rows = jnp.zeros((128, 1), F32)
    for n in range(18):
        here = slice(128 * n, 128 * n + 128)
        grad = ffn_grads[:, here]
        out[1040 + 128 * n : 1168 + 128 * n, :] = grad
        if n % 6 < 4:
            rows = rows + jnp.sum(grad.astype(F32) * ffn_weights[:, here].astype(F32), 1, keepdims=True)
    sums[1:2, :] = rows.reshape(1, 128)


def ffn_kernel(source, *refs):
    parts, grads, stored, (active, back, second), (kept, weights, sems) = refs[:2], refs[2:4], refs[4], refs[5:8], refs[8:]
    step = pl.program_id(0)

    def copy(j):
        return pltpu.make_async_copy(stored.at[:, pl.ds(j * 768, 768)], weights.at[j], sems.at[j])

    @pl.when(step == 0)
    def _():
        for j in range(3):
            copy(j).start()

    for j in range(3):

        @pl.when(step == j)
        def _():
            copy(j).wait()
            for n, (part, grad) in enumerate(zip(parts, grads)):
                here = slice(n * 512, n * 512 + 512)
                both = dot(part[...], weights[j, :, :512], NN)
                grad_active = dot(grad[...], weights[j, :, 512:], NN)
                gate, up = both[:, :256], both[:, 256:]
                sigma = sigmoid(gate)
                swish = gate * sigma
                active[here, :] = (swish * up).astype(BF16)
                slope = sigma * (1.0 + gate * (1.0 - sigma))
                backs = jnp.concatenate([grad_active * up * slope, grad_active * swish], 1).astype(BF16)
                back[here, :] = backs
                kept[here, j * 512 : j * 512 + 512] = backs

    @pl.when(step == 2)
    def _():
        every = jnp.concatenate([weights[j, :, :512] for j in range(3)], 1)
        for n in range(2):
            done = dot(kept[n * 512 : n * 512 + 512, :], every, NT).astype(BF16)
            for q in range(4):
                second[spot(source, n * 4 + q), :] = done[q * C : q * C + C]


def ffn(source, parts, grads, weights):
    whole = [pl.BlockSpec((512, D), lambda j, source: (0, 0))] * 4
    return pl.pallas_call(
        ffn_kernel,
        grid_spec=pltpu.PrefetchScalarGridSpec(
            num_scalar_prefetch=1,
            grid=(3,),
            in_specs=whole + [pl.BlockSpec(memory_space=pl.ANY)],
            out_specs=[
                pl.BlockSpec((1024, 256), lambda j, source: (0, j)),
                pl.BlockSpec((1024, 512), lambda j, source: (0, j)),
                pl.BlockSpec((1024, D), lambda j, source: (0, 0)),
            ],
            scratch_shapes=[
                pltpu.VMEM((1024, 1536), BF16),
                pltpu.VMEM((3, D, 768), BF16),
                pltpu.SemaphoreType.DMA((3,)),
            ],
        ),
        out_shape=[
            jax.ShapeDtypeStruct((1024, 768), BF16),
            jax.ShapeDtypeStruct((1024, 1536), BF16),
            jax.ShapeDtypeStruct((1024, D), BF16),
        ],
        compiler_params=pltpu.CompilerParams(vmem_limit_bytes=60 * 1024 * 1024),
        cost_estimate=pl.CostEstimate(flops=2 * 1024 * D * 1280 * 3, bytes_accessed=30 << 20, transcendentals=0),
        name="ffn",
    )(source, *parts, *grads, weights)


def ffn_grad_kernel(*refs):
    parts, grads, (back, active, out) = refs[:2], refs[2:4], refs[4:]
    seq = jnp.concatenate([ref[...].T for ref in parts], 1)
    dy = jnp.concatenate([ref[...].T for ref in grads], 1)
    for j in range(3):
        at = j * 768
        out[:, at : at + 512] = dot(seq, back[:, j * 512 : j * 512 + 512], NN).astype(BF16)
        out[:, at + 512 : at + 768] = dot(dy, active[:, j * 256 : j * 256 + 256], NN).astype(BF16)


def ffn_grad(parts, grads, back, active):
    block = 512
    return pl.pallas_call(
        ffn_grad_kernel,
        grid=(D // block,),
        in_specs=[pl.BlockSpec((part.shape[0], block), lambda i: (0, i)) for part in (*parts, *grads)]
        + [pl.BlockSpec(part.shape, lambda i: (0, 0)) for part in (back, active)],
        out_specs=pl.BlockSpec((block, 2304), lambda i: (i, 0)),
        out_shape=jax.ShapeDtypeStruct((D, 2304), BF16),
        compiler_params=pltpu.CompilerParams(vmem_limit_bytes=60 * 1024 * 1024),
        cost_estimate=pl.CostEstimate(flops=2 * 1024 * D * 2304, bytes_accessed=20 << 20, transcendentals=0),
        name="ffn_grad",
    )(*parts, *grads, back, active)


def in_grad_kernel(one, back, taps, near, other, mixed, out):
    total = dot(one[...], back[...], NN)
    outer = 0.0
    at = 0
    for ref in (near, other):
        outer = outer + dot(mixed[at : at + ref.shape[0], :].T, ref[...], NN)
        at += ref.shape[0]
    small = total[:, 768:].T
    every = jnp.concatenate([taps[...], jnp.zeros((96, C), F32)], 0).astype(BF16)
    lane = lax.broadcasted_iota(jnp.int32, (8, C), 1)
    for r in range(4):
        rows = slice(r * 128, r * 128 + 128)
        for n in range(6):
            out[r, n * 128 : n * 128 + 128, :] = total[rows, n * 128 : n * 128 + 128].astype(BF16)
        chosen = lane == place_of(pl.program_id(0) * 4 + r) * 8 + lax.broadcasted_iota(jnp.int32, (8, C), 0)
        picked = dot(jnp.where(chosen, 1.0, 0.0).astype(BF16), every, NT)
        tail = jnp.concatenate([small[:2, rows], picked, jnp.zeros((6, 128), F32)], 0)
        out[r, 768:784, :] = tail.astype(BF16)
        out[r, 784:, :] = outer[:, rows].astype(BF16)


def in_grad(one, back, taps, three, mixed):
    block = 512
    return pl.pallas_call(
        in_grad_kernel,
        grid=(D // block,),
        in_specs=[
            pl.BlockSpec((block, 1024), lambda i: (i, 0)),
            pl.BlockSpec(back.shape, lambda i: (0, 0)),
            pl.BlockSpec((32, C), lambda i: (0, 0)),
            *[pl.BlockSpec((part.shape[0], block), lambda i: (0, i)) for part in three],
            pl.BlockSpec(mixed.shape, lambda i: (0, 0)),
        ],
        out_specs=pl.BlockSpec((4, 1040, 128), lambda i: (i, 0, 0)),
        out_shape=jax.ShapeDtypeStruct((16, 1040, 128), BF16),
        compiler_params=pltpu.CompilerParams(vmem_limit_bytes=60 * 1024 * 1024),
        cost_estimate=pl.CostEstimate(flops=2 * 1024 * D * 1152, bytes_accessed=8 << 20, transcendentals=0),
        name="in_grad",
    )(one, back, taps, *three, mixed)


def first_kernel_parts(back, weights, *outs):
    at = 0
    for out in outs:
        count = out.shape[0]
        out[...] = dot(back[at : at + count, :], weights[...], NT).astype(BF16)
        at += count


def first_parts(back, weights):
    block = 512
    return pl.pallas_call(
        first_kernel_parts,
        grid=(D // block,),
        in_specs=[pl.BlockSpec((1024, 896), lambda i: (0, 0)), pl.BlockSpec((block, 896), lambda i: (i, 0))],
        out_specs=[pl.BlockSpec((count, block), lambda i: (0, i)) for count in PARTS],
        out_shape=[jax.ShapeDtypeStruct((count, D), BF16) for count in PARTS],
        compiler_params=pltpu.CompilerParams(vmem_limit_bytes=60 * 1024 * 1024),
        cost_estimate=pl.CostEstimate(flops=2 * 1024 * D * 896, bytes_accessed=8 << 20, transcendentals=0),
        name="first_parts",
    )(back, weights)


def down_kernel(active, first, second, third, wait, *outs):
    right = jnp.concatenate([first[...], second[...], third[...]], 1)
    at = 0
    for out in outs:
        out[...] = dot(active[at : at + out.shape[0], :], right, NT).astype(BF16)
        at += out.shape[0]


def down_product(active, weights, wait):
    block = 512
    return pl.pallas_call(
        down_kernel,
        grid=(D // block,),
        in_specs=[pl.BlockSpec((1024, PAD), lambda i: (0, 0))]
        + [pl.BlockSpec((block, 256), lambda i, j=j: (i, 3 * j + 2)) for j in range(3)]
        + [pl.BlockSpec(memory_space=pl.ANY)],
        out_specs=[pl.BlockSpec((count, block), lambda i: (0, i)) for count in PARTS],
        out_shape=[jax.ShapeDtypeStruct((count, D), BF16) for count in PARTS],
        compiler_params=pltpu.CompilerParams(vmem_limit_bytes=60 * 1024 * 1024),
        cost_estimate=pl.CostEstimate(flops=2 * 1024 * D * 768, bytes_accessed=8 << 20, transcendentals=0),
        name="down_product",
    )(active, weights, weights, weights, wait)


def team_total(values):
    values = values.reshape(2, 4, 2, 16)
    core = lax.axis_index("c")
    mine = lax.dynamic_index_in_dim(values, core, 2, False)
    mine = mine + mate(lax.dynamic_index_in_dim(values, 1 - core, 2, False))
    place = lax.axis_index("z")
    total = 0.0
    for distance in range(4):
        block = lax.dynamic_index_in_dim(mine, (place + distance) & 3, 1, False)
        pairs = [
            ((c * 4 + n) * 2 + y, (y * 4 + (n + distance) % 4) * 2 + c)
            for c in range(2)
            for n in range(4)
            for y in range(2)
        ]
        total = total + lax.ppermute(block, ("c", "z", "yl"), pairs)
    return total


def on_device(
    tokens,
    segments,
    cotangent,
    attn_gain,
    w_query,
    w_key,
    w_value,
    w_beta,
    conv_weight,
    w_out,
    ffn_gain,
    w_gate,
    w_up,
    w_down,
):
    core, z = lax.axis_index("c"), lax.axis_index("z")
    true = jnp.arange(8, dtype=jnp.int32)
    distance, other = (true // 2 - z) & 3, (true % 2) ^ core
    place = (jnp.where(distance > 1, 5 - distance, distance) + 4 * other).astype(jnp.int32)

    source = jnp.sum(jnp.where(place[:, None] == true[None, :], true[:, None], 0), 0).astype(jnp.int32)

    mix_pack, gains = local_call(
        mix_pack_kernel,
        "mix_pack",
        [((128, 1152 + D), BF16), ((16, 2, 16), F32)],
        w_query,
        w_key,
        w_value,
        w_beta.T,
        conv_weight.reshape(24, 8),
        segments.reshape(8, 128),
        w_out,
        attn_gain.reshape(1, 16),
        ffn_gain.reshape(1, 16),
        tokens,
        limit=60,
    )
    mix_pack = trade(mix_pack)
    rows, one = local_call(norm_kernel, "norm_one", [((128, D), BF16)] * 2, mix_pack)
    (grad_rows,) = local_call(order_kernel, "order_grad", [((128, D), BF16)], cotangent, limit=60)
    grad_rows = trade(grad_rows)
    (ffn_pack,) = local_call(ffn_pack_kernel, "ffn_pack", [((128, 2304), BF16)], w_gate.T, w_up.T, w_down, limit=60)
    ffn_pack = trade(ffn_pack)

    gains = lax.all_to_all(gains, ("z", "yl", "c"), 0, 0, tiled=True).reshape(8, 2, 2, 16)
    gains = gains.transpose(1, 2, 0, 3).reshape(2, 2, 128)
    home = jnp.where(core == 0, gains[0], gains[1])
    away = jnp.where(lax.axis_index("yl") == 0, gains[0], gains[1])
    (scaled_pack,) = local_call(mix_scale_kernel, "mix_scale", [((128, 1152), BF16)], mix_pack, away[0][:, None])
    mix_w = gather_ring(scaled_pack)

    one = gather_team(one)
    grads = gather_team(grad_rows)
    (scaled_ffn,) = local_call(
        ffn_scale_kernel, "ffn_scale", [((128, 2304), BF16)], ffn_pack, away[1][:, None]
    )
    ffn_w = gather_ring(scaled_ffn)

    marks, seg_rows = local_call(marks_kernel, "marks", [((1024, 128), F32), ((8, 128), F32)], mix_pack)
    mixed, raw, taps, *saved = mix_forward(place, one, mix_w, marks, seg_rows, (scaled_ffn, grads[1]))
    middle, two = local_call(
        middle_kernel, "middle", [((128, D), F32), ((128, D), BF16)], rows, *sum_team(*saved[:2])
    )
    one_turned = turned(one, saved[0])
    two = gather_team(two)
    active, ffn_back, second = ffn(source, two, grads, ffn_w)
    ffn_grads = ffn_grad(two, grads, ffn_back, active)
    result = down_product(active, ffn_w, second)
    middle_grad, three = local_call(
        second_kernel,
        "second",
        [((128, D), F32), ((128, D), BF16)],
        middle,
        grad_rows,
        sum_rows(second),
        waits=(ffn_grads, one_turned, result[0]),
        limit=60,
    )
    ring_grads = lax.psum_scatter(ffn_grads, RING, scatter_dimension=0, tiled=True)
    three = gather_team(three)
    back, taps_grad = mix_backward(place, three, mix_w, raw, taps, marks, seg_rows, saved[2:])
    ring_parts = lax.all_to_all(in_grad(one_turned, back, taps_grad, three, mixed), RING, 0, 0, tiled=True)
    terms = sum_team(*first_parts(back, mix_w))
    (tokens_grad,) = local_call(first_kernel, "first", [((128, D), BF16)], rows, middle_grad, *terms)
    (tokens_grad,) = local_call(widen_kernel, "widen", [((128, D), F32)], trade(tokens_grad))
    terms = sum_team(*result, waits=terms[:1])
    (output,) = local_call(result_kernel, "result", [((128, D), BF16)], middle, *terms)
    output = trade(output)
    total, sums = local_call(
        total_kernel,
        "ring_total",
        [((1040 + 2304, 128), BF16), ((2, 128), F32)],
        ring_parts,
        scaled_pack,
        ring_grads,
        scaled_ffn,
        waits=(tokens_grad, output),
        limit=60,
    )
    total, sums = trade(total), team_total(sums)
    grad_gate, grad_up, grad_down = local_call(
        ffn_unpack_kernel, "ffn_unpack", [((HID, 128), F32)] * 3, total, home[1][None]
    )
    grad_query, grad_key, grad_value, grad_beta, grad_taps, grad_out = local_call(
        mix_unpack_kernel,
        "mix_unpack",
        [((128, 256), F32)] * 3 + [((2, 128), F32), ((8, 128), F32), ((256, 128), F32)],
        total,
        home[0][:, None],
    )
    grad_taps = grad_taps[:, :24].reshape(8, 3, 4, 2).transpose(1, 2, 3, 0)
    return (
        output,
        tokens_grad,
        sums[0] / attn_gain,
        grad_query,
        grad_key,
        grad_value,
        grad_beta.T,
        grad_taps,
        grad_out,
        sums[1] / ffn_gain,
        grad_gate.T,
        grad_up.T,
        grad_down,
    )


def solution(mesh):
    dp, tensor = ("yh", "x", "c"), ("z", "yl")
    every = dp + tensor
    split = jax.sharding.Mesh(mesh.devices.reshape(2, 4, 2, 4, 2), AXES)
    placed = (
        P(every, None),
        P(dp),
        P(every, None),
        P(every),
        P(dp, tensor),
        P(dp, tensor),
        P(dp, tensor),
        P(dp, tensor),
        P(None, None, tensor, dp),
        P(tensor, dp),
        P(every),
        P(dp, tensor),
        P(dp, tensor),
        P(tensor, dp),
    )
    return jax.shard_map(
        on_device,
        mesh=split,
        in_specs=placed,
        out_specs=(
            P(every, None),
            P(every, None),
            P(every),
            P(dp, tensor),
            P(dp, tensor),
            P(dp, tensor),
            P(dp, tensor),
            P(None, None, tensor, dp),
            P(tensor, dp),
            P(every),
            P(dp, tensor),
            P(dp, tensor),
            P(tensor, dp),
        ),
        check_vma=False,
    )
```
